32 devices in a mesh: fsdp: 2 (over x), ctx: 4 (over z), tp: 4 (over y, core).
Axes of the slice: x: 2, y: 2, z: 4, core: 2. Of those that a mesh axis runs over, the one named last changes fastest.
Arguments:
- frames: bfloat16 [2, 1536, 768], P('fsdp', 'ctx'), may hold values from -6 to 6
- w_qkv: bfloat16 [3, 768, 768], P(None, ('fsdp', 'ctx'), 'tp'), may hold values from -0.3125 to 0.3125
- w_out: bfloat16 [768, 768], P('tp', ('fsdp', 'ctx')), may hold values from -0.875 to 0.875
- w_fc1: bfloat16 [768, 3072], P(('fsdp', 'ctx'), 'tp'), may hold values from -0.21875 to 0.21875
- w_fc2: bfloat16 [3072, 768], P('tp', ('fsdp', 'ctx')), may hold values from -0.109375 to 0.109375
- head_bias: bfloat16 [4, 384], P('tp', ('fsdp', 'ctx')), may hold values from -3 to 3
- hidden_bias: bfloat16 [4, 768], P('tp', ('fsdp', 'ctx')), may hold values from -3 to 3
- ln_gain: bfloat16 [2, 768], P(None, ('fsdp', 'ctx')), may hold values from 0.099609375 to 1.8984375
- ln_bias: bfloat16 [2, 768], P(None, ('fsdp', 'ctx')), may hold values from -2 to 2
- out_bias: bfloat16 [2, 768], P(None, ('fsdp', 'ctx')), may hold values from -2 to 2
- cotangent: bfloat16 [2, 1536, 768], P('fsdp', 'ctx'), may hold values from -6 to 6
Outputs:
- output: bfloat16 [2, 1536, 768], P('fsdp', 'ctx')
- input_grad: bfloat16 [2, 1536, 768], P('fsdp', 'ctx')
- grad_qkv: float32 [3, 768, 768], P(None, ('fsdp', 'ctx'), 'tp')
- grad_out: float32 [768, 768], P('tp', ('fsdp', 'ctx'))
- grad_fc1: float32 [768, 3072], P(('fsdp', 'ctx'), 'tp')
- grad_fc2: float32 [3072, 768], P('tp', ('fsdp', 'ctx'))
- grad_head_bias: float32 [4, 384], P('tp', ('fsdp', 'ctx'))
- grad_hidden_bias: float32 [4, 768], P('tp', ('fsdp', 'ctx'))
- grad_ln_gain: float32 [2, 768], P(None, ('fsdp', 'ctx'))
- grad_ln_bias: float32 [2, 768], P(None, ('fsdp', 'ctx'))
- grad_out_bias: float32 [2, 768], P(None, ('fsdp', 'ctx'))
The draws below stay inside these ranges and needn't reach their ends.
All inputs are finite; a program needn't handle non-finite values.
Results may differ from the reference program's by a relative error of at most 0.018.
The reference program's roundings to bfloat16 on the way count: a program that leaves them out, or rounds other values in their place, can miss the bound.
Values may be sent and summed in bfloat16 or wider, within the bound.
No kernel may reach another device: no remote copies, remote signals or barrier semaphores. Data moves between devices by JAX's collectives and lax.ppermute only.
A program may use at most 128 MiB of HBM per device.

```python
import jax
import jax.numpy as jnp
from jax import lax

D = 768
H = 12
DH = 64
FF = 3072
CLIP_LEN = 1536
CLIPS = 2
N_TP = 4


def levels(own_key, extent, split, low, largest):
    def one(axis_at, shards_of):
        heights = jax.random.uniform(jax.random.fold_in(jax.random.fold_in(own_key, 6), axis_at), (shards_of,), jnp.float32, low / len(split), largest / len(split))
        return jnp.repeat(jnp.exp(heights), extent[axis_at] // shards_of).reshape((-1,) + (1,) * (len(extent) - axis_at - 1))

    factor_of = one(*split[0])
    for cut in split[1:]:
        factor_of = factor_of * one(*cut)
    return factor_of


def gaussian(stream_key, extent, scale, limit, split=(), kind=jnp.bfloat16):
    entries = jax.random.normal(stream_key, extent, jnp.float32) * scale
    if len(split) > 0:
        entries = levels(stream_key, extent, split, -0.22, 0.18) * entries
    return jnp.clip(entries, min=-limit, max=limit).astype(kind)


def setup_inputs(seed: int = 0) -> dict:
    keys = jax.random.split(jax.random.key(seed), 12)
    return {
        "frames": gaussian(keys[0], (CLIPS, CLIP_LEN, D), 1.0, 6.0, ((0, 2), (1, 4))),
        "w_qkv": gaussian(keys[1], (3, D, D), (D // 2) ** -0.5, 0.3125, ((1, 8), (2, 4))),
        "w_out": gaussian(keys[2], (D, D), (D // 16) ** -0.5, 0.875, ((0, 4), (1, 8))),
        "w_fc1": gaussian(keys[3], (D, FF), D ** -0.5, 0.21875, ((0, 8), (1, 4))),
        "w_fc2": gaussian(keys[4], (FF, D), FF ** -0.5, 0.109375, ((0, 4), (1, 8))),
        "head_bias": gaussian(keys[5], (N_TP, 2 * D // N_TP), 0.5, 3.0, ((0, 4), (1, 8))),
        "hidden_bias": gaussian(keys[6], (N_TP, FF // N_TP), 0.5, 3.0, ((0, 4), (1, 8))),
        "ln_gain": jnp.clip(1.0 + 0.18 * jax.random.normal(keys[7], (2, D), jnp.float32), 0.099609375, 1.8984375).astype(jnp.bfloat16),
        "ln_bias": gaussian(keys[8], (2, D), 0.3, 2.0, ((1, 8),)),
        "out_bias": gaussian(keys[9], (2, D), 0.3, 2.0, ((1, 8),)),
        "cotangent": gaussian(keys[10], (CLIPS, CLIP_LEN, D), 1.0, 6.0, ((0, 2), (1, 4))),
    }


epsilon = 1e-05

@jax.custom_vjp
def low(v):
    return lax.optimization_barrier(v.astype(jnp.bfloat16)).astype(jnp.float32)

@jax.custom_vjp
def low_back(v):
    return v

def low_keep(v):
    return (low(v), None)

def low_pass(kept, grad):
    return (grad,)

def back_keep(v):
    return (v, None)

def back_low(kept, grad):
    return (low(grad),)
low.defvjp(low_keep, low_pass)
low_back.defvjp(back_keep, back_low)

def layer_norm(values, gain, shift_term):
    average = lax.optimization_barrier(jnp.mean(values, axis=-1, keepdims=True))
    centered = values - average
    variance = lax.optimization_barrier(jnp.mean(centered * centered, axis=-1, keepdims=True))
    return centered * lax.rsqrt(variance + epsilon) * gain + shift_term

def product(left, right, form):
    return jnp.einsum(form, left, right, precision=lax.Precision.HIGHEST)

def encoder_layer(clip, w_qkv, w_out, w_fc1, w_fc2, head_bias, hidden_bias, ln_gain, ln_bias, out_bias):
    length = clip.shape[0]
    local_width = head_bias.shape[1] // 2
    query_bias = head_bias[:, :local_width].reshape(-1)
    value_bias = head_bias[:, local_width:].reshape(-1)
    normed = low(layer_norm(clip, ln_gain[0], ln_bias[0]))
    projected = product(normed, w_qkv, 'td,kde->kte')
    queries = low(low_back(projected[0] + query_bias)).reshape(length, H, DH)
    keys_all = low(low_back(projected[1])).reshape(length, H, DH)
    values_all = low(low_back(projected[2] + value_bias)).reshape(length, H, DH)
    scores = low_back(product(queries, keys_all, 'qhd,khd->hqk') * DH ** (-0.5))
    probs = low(jax.nn.softmax(scores, axis=-1))
    attended = low(low_back(product(probs, values_all, 'hqk,khd->qhd').reshape(length, H * DH)))
    branch = low_back(product(attended, w_out, 'te,ed->td') + out_bias[0])
    middle = clip + branch
    normed_two = low(layer_norm(middle, ln_gain[1], ln_bias[1]))
    hidden = low_back(product(normed_two, w_fc1, 'td,df->tf') + hidden_bias.reshape(-1))
    activated = low(jax.nn.gelu(hidden, approximate=False))
    return middle + product(activated, w_fc2, 'tf,fd->td') + out_bias[1]

def reference(frames, w_qkv, w_out, w_fc1, w_fc2, head_bias, hidden_bias, ln_gain, ln_bias, out_bias, cotangent):
    params = (w_qkv.astype(jnp.float32), w_out.astype(jnp.float32), w_fc1.astype(jnp.float32), w_fc2.astype(jnp.float32), head_bias.astype(jnp.float32), hidden_bias.astype(jnp.float32), ln_gain.astype(jnp.float32), ln_bias.astype(jnp.float32), out_bias.astype(jnp.float32))

    def one_clip(running, pair):
        clip, clip_grad = pair
        result, pull = jax.vjp(encoder_layer, clip.astype(jnp.float32), *params)
        grads = pull(clip_grad.astype(jnp.float32))
        running = tuple((carried + fresh for carried, fresh in zip(running, grads[1:])))
        return (running, (result.astype(jnp.bfloat16), grads[0].astype(jnp.bfloat16)))
    start = tuple((jnp.zeros(param.shape, jnp.float32) for param in params))
    summed, (outputs, input_grad) = lax.scan(one_clip, start, (frames, cotangent))
    return (outputs, input_grad, summed[0], summed[1], summed[2], summed[3], summed[4], summed[5], summed[6], summed[7], summed[8])
```

```python
import functools

import jax
import jax.numpy as jnp
from jax import lax
from jax.experimental import pallas as pl
from jax.experimental.pallas import tpu as pltpu
from jax.sharding import PartitionSpec as P

DH = 64
EPS = 1e-05
BF = jnp.bfloat16
F32 = jnp.float32
LANES = 256
DELTA = 192
LSE = 224
PIECES = 3
VMEM_LIMIT = 56 * 1024 * 1024


def ring(axis, k):
    n = lax.axis_size(axis)
    return [(i, (i + k) % n) for i in range(n)]


def send(x, axis, k):
    return lax.ppermute(x, axis, ring(axis, k))


def flip(x, axis, bit):
    return lax.ppermute(x, axis, [(i, i ^ bit) for i in range(lax.axis_size(axis))])


def tp_sum(both):
    got = flip(both[1], "tp", 1)
    half = (both[0].astype(F32) + got.astype(F32)).astype(BF)
    bit = 2
    while bit < lax.axis_size("tp"):
        far = flip(half, "tp", bit)
        half = (half.astype(F32) + far.astype(F32)).astype(BF)
        bit *= 2
    return half, flip(half, "tp", 1)


def gather_blocks(x):
    near = [x] + [send(x, "ctx", k) for k in range(1, lax.axis_size("ctx"))]
    near = jnp.stack(near)
    return jnp.stack([near] + [send(near, "fsdp", k) for k in range(1, lax.axis_size("fsdp"))])


def reduce_blocks(blocks):
    total = blocks[0].astype(F32)
    for k in range(1, lax.axis_size("fsdp")):
        total = total + send(blocks[k], "fsdp", k).astype(F32)
    low = total.astype(BF)
    total = low[0].astype(F32)
    for k in range(1, lax.axis_size("ctx")):
        total = total + send(low[k], "ctx", k).astype(F32)
    return total


def turned(x, shift, axis):
    n = x.shape[axis]
    return jnp.take(x, (shift - jnp.arange(n)) % n, axis=axis)


def canonical(blocks):
    return turned(turned(blocks, lax.axis_index("fsdp"), 0), lax.axis_index("ctx"), 1)


def relative(blocks):
    f, c = lax.axis_index("fsdp"), lax.axis_index("ctx")
    blocks = jnp.take(blocks, (f + jnp.arange(blocks.shape[0])) % blocks.shape[0], axis=0)
    return jnp.take(blocks, (c + jnp.arange(blocks.shape[1])) % blocks.shape[1], axis=1)


def dot(a, b, da, db):
    return lax.dot_general(a, b, (((da,), (db,)), ((), ())), preferred_element_type=F32)


def nn(a, b):
    return dot(a, b, 1, 0)


def nt(a, b):
    return dot(a, b, 1, 1)


def tn(a, b):
    return dot(a, b, 0, 0)


def lanes_of(rows):
    return lax.broadcasted_iota(jnp.int32, (rows, LANES), 1)


def head_lanes(lane, h):
    return (lane >= h * DH) & (lane < (h + 1) * DH)


def piece_lanes(lane, first, h):
    return (lane >= first + PIECES * h) & (lane < first + PIECES * (h + 1))


def in_pieces(lane, first, h, column):
    out = jnp.zeros(lane.shape, F32)
    rest = column
    for j in range(PIECES):
        piece = rest.astype(BF).astype(F32)
        out = jnp.where(lane == first + PIECES * h + j, piece, out)
        rest = rest - piece
    return out


def normalized(x):
    mean = jnp.mean(x, axis=-1, keepdims=True)
    centered = x - mean
    var = jnp.mean(centered * centered, axis=-1, keepdims=True)
    rstd = lax.rsqrt(var + EPS)
    return centered * rstd, rstd


def norm_back(grad, gain, xhat, rstd):
    dx = grad * gain
    return rstd * (
        dx
        - jnp.mean(dx, axis=-1, keepdims=True)
        - xhat * jnp.mean(dx * xhat, axis=-1, keepdims=True)
    )


def column_sum(x):
    return jnp.sum(x, axis=0, keepdims=True)


def call(kernel, outs, *args, scratch=(), flops=0, idx=None):
    ins = [pl.BlockSpec(memory_space=pltpu.VMEM) for _ in args]
    if idx is not None:
        ins = [pl.BlockSpec(memory_space=pltpu.SMEM)] + ins
        args = (idx, *args)
    moved = sum(a.size * a.dtype.itemsize for a in args)
    moved += sum(o.size * o.dtype.itemsize for o in outs)
    return pl.pallas_call(
        kernel,
        out_shape=tuple(outs),
        in_specs=ins,
        out_specs=tuple(pl.BlockSpec(memory_space=pltpu.VMEM) for _ in outs),
        scratch_shapes=list(scratch),
        compiler_params=pltpu.CompilerParams(vmem_limit_bytes=VMEM_LIMIT),
        cost_estimate=pl.CostEstimate(flops=flops, bytes_accessed=moved, transcendentals=0),
    )(*args)


def shape(*dims, dtype=BF):
    return jax.ShapeDtypeStruct(dims, dtype)


def arrange_kernel(rows, idx, *refs):
    ins, (w_ref, small_ref) = refs[:-2], refs[-2:]
    f, c = idx[0], idx[1]
    n_f, n_c = len(ins), ins[0].shape[0]
    for a in range(n_f):
        for b in range(n_c):
            at = lax.rem(f - a + n_f, n_f) * n_c + lax.rem(c - b + n_c, n_c)
            w_ref[pl.ds(pl.multiple_of(at * rows, rows), rows), :] = ins[a][b, :rows, :]
            if ins[a].shape[1] > rows:
                small_ref[pl.ds(at, 1)] = ins[a][b, rows:, :][None]
            else:
                small_ref[pl.ds(at, 1)] = ins[a][b, :16, :][None]


def arrange(parts, rows, idx):
    n_c, total, width = parts[0].shape
    blocks = len(parts) * n_c
    if rows % 16 == 0:
        extra = max(total - rows, 16)
        return call(
            functools.partial(arrange_kernel, rows),
            (shape(blocks * rows, width), shape(blocks, extra, width)),
            *parts,
            idx=idx,
        )
    whole = canonical(jnp.stack(parts)).reshape(blocks, total, width)
    return whole[:, :rows].reshape(blocks * rows, width), whole[:, rows:]


def place_blocks(full_ref, out_ref, idx, rows):
    f, c = idx[0], idx[1]
    n_f, n_c = out_ref.shape[:2]
    for a in range(n_f):
        for b in range(n_c):
            at = lax.rem(f + a, n_f) * n_c + lax.rem(c + b, n_c)
            out_ref[a, b] = full_ref[pl.ds(pl.multiple_of(at * rows, rows), rows), :]


def attend_kernel(
    idx, own_ref, far_ref, w_ref, wo_ref, vec_ref, hb_ref,
    n1_ref, q_ref, k_ref, v_ref, o_ref, aux_ref, br_ref,
):
    length = own_ref.shape[0]
    total = length + far_ref.shape[0]
    heads = DELTA // DH
    step = 128
    gain, shift = vec_ref[0:1, :], vec_ref[2:3, :]
    lane = lanes_of(step)

    def project(x, at):
        xhat, _ = normalized(x.astype(F32))
        n1 = (xhat * gain + shift).astype(BF)
        qkv = nn(n1, w_ref[...])
        q = (qkv[:, :LANES] + hb_ref[0:1, :]).astype(BF)
        k = qkv[:, LANES : 2 * LANES].astype(BF)
        v = (qkv[:, 2 * LANES :] + hb_ref[1:2, :]).astype(BF)
        here = pl.ds(at, step)
        q_ref[here, :] = jnp.where(lane < DELTA, q * jnp.asarray(DH**-0.5, BF), jnp.zeros_like(q))
        k_ref[here, :] = jnp.where(lane < DELTA, k, jnp.ones_like(k))
        v_ref[here, :] = jnp.where(lane < DELTA, v, jnp.ones_like(v))
        return n1

    @pl.loop(0, length // step)
    def _(i):
        at = pl.multiple_of(i * step, step)
        n1_ref[pl.ds(at, step), :] = project(own_ref[pl.ds(at, step), :], at)

    @pl.loop(0, (total - length) // step)
    def _(i):
        at = pl.multiple_of(i * step, step)
        project(far_ref[pl.ds(at, step), :], pl.multiple_of(at + length, step))

    rows = length // 4
    lane = lanes_of(rows)

    @pl.loop(0, 4)
    def _(i):
        here = pl.ds(pl.multiple_of(i * rows, rows), rows)
        q = q_ref[here, :]
        out = jnp.zeros((rows, LANES), F32)
        aux = jnp.zeros((rows, LANES), F32)
        for h in range(heads):
            mask = head_lanes(lane, h)
            s = nt(jnp.where(mask, q, jnp.zeros_like(q)), k_ref[...])
            top = jnp.max(s, axis=-1, keepdims=True)
            e = jnp.exp(s - top)
            ev = nn(e.astype(BF), v_ref[...])
            mass = ev[:, DELTA : DELTA + 1]
            out = jnp.where(mask, ev / mass, out)
            aux = aux + in_pieces(lane, LSE, h, -(top + jnp.log(mass)))
        o_ref[here, :] = out
        aux_ref[here, :] = aux.astype(BF)
        br_ref[
            pl.ds(lax.rem(i // 2 + idx[2], 2), 1), pl.ds(pl.multiple_of(lax.rem(i, 2) * rows, rows), rows), :
        ] = nt(out.astype(BF), wo_ref[...]).astype(BF)[None]


def summed(idx, i, rows, mine_ref, other_ref):
    here = pl.ds(pl.multiple_of(lax.rem(i, 2) * rows, rows), rows)
    is_mine = (i // 2) == idx[2]
    return jnp.where(is_mine, mine_ref[here, :].astype(F32), other_ref[here, :].astype(F32))


def put_halves(idx, i, rows, out_ref, value):
    out_ref[
        pl.ds(lax.rem(i // 2 + idx[2], 2), 1), pl.ds(pl.multiple_of(lax.rem(i, 2) * rows, rows), rows), :
    ] = value[None]


def feed_kernel(
    idx, x_ref, a_ref, b_ref, c_ref, w1_ref, w2_ref, vec_ref,
    m_ref, n2_ref, g_ref, df_ref, mlp_ref, dn_ref,
):
    rows = x_ref.shape[0] // 4
    gain, shift, outb, hidb = vec_ref[1:2, :], vec_ref[3:4, :], vec_ref[4:5, :], vec_ref[6:7, :]

    @pl.loop(0, 4)
    def _(i):
        here = pl.ds(pl.multiple_of(i * rows, rows), rows)
        m = x_ref[here, :].astype(F32) + (summed(idx, i, rows, a_ref, b_ref) + outb)
        m_ref[here, :] = m
        xhat, _ = normalized(m)
        n2 = (xhat * gain + shift).astype(BF)
        n2_ref[here, :] = n2
        f = nn(n2, w1_ref[...]) + hidb
        cdf = 0.5 * (1.0 + lax.erf(f * (0.5**0.5)))
        g = (f * cdf).astype(BF)
        g_ref[here, :] = g
        dg = nn(c_ref[here, :], w2_ref[...])
        slope = cdf + f * (jnp.exp(-0.5 * f * f) * 0.3989422804014327)
        df = (dg * slope).astype(BF)
        df_ref[here, :] = df
        put_halves(idx, i, rows, dn_ref, nt(df, w1_ref[...]).astype(BF))
        put_halves(idx, i, rows, mlp_ref, nt(g, w2_ref[...]).astype(BF))


def feed_grad_kernel(rel, idx, n2_ref, df_ref, c_ref, g_ref, g1_ref, g2_ref, hid_ref, full1, full2):
    hid_ref[...] = column_sum(df_ref[...].astype(F32))
    step = 128
    if not rel:
        full1, full2 = g1_ref, g2_ref

    @pl.loop(0, n2_ref.shape[1] // step)
    def _(i):
        here = pl.ds(pl.multiple_of(i * step, step), step)
        full1[here, :] = tn(n2_ref[:, here], df_ref[...]).astype(BF)
        full2[here, :] = tn(c_ref[:, here], g_ref[...]).astype(BF)

    if rel:
        place_blocks(full1, g1_ref, idx, g1_ref.shape[2])
        place_blocks(full2, g2_ref, idx, g2_ref.shape[2])


def middle_kernel(
    idx, m_ref, a_ref, b_ref, c_ref, o_ref, aux_ref, wo_ref, vec_ref,
    dm_ref, da_ref, pay_ref, sums_ref,
):
    rows = m_ref.shape[0] // 4
    heads = DELTA // DH
    gain = vec_ref[1:2, :]
    lane = lanes_of(rows)
    sums_ref[...] = jnp.zeros_like(sums_ref)

    @pl.loop(0, 4)
    def _(i):
        here = pl.ds(pl.multiple_of(i * rows, rows), rows)
        xhat, rstd = normalized(m_ref[here, :])
        dn = summed(idx, i, rows, a_ref, b_ref)
        c = c_ref[here, :].astype(F32)
        dm = c + norm_back(dn, gain, xhat, rstd)
        dm_ref[here, :] = dm
        da = dm.astype(BF)
        da_ref[here, :] = da
        do = nn(da, wo_ref[...]).astype(BF)
        prod = do.astype(F32) * o_ref[here, :]
        extra = aux_ref[here, :].astype(F32)
        for h in range(heads):
            delta = jnp.sum(jnp.where(head_lanes(lane, h), prod, 0.0), axis=-1, keepdims=True)
            extra = extra + in_pieces(lane, DELTA, h, -delta)
        pay_ref[here, :] = jnp.where(lane < DELTA, do, extra.astype(BF))
        sums_ref[0:1, :] += column_sum(dn * xhat)
        sums_ref[1:2, :] += column_sum(dn)
        sums_ref[2:3, :] += column_sum(da.astype(F32))
        sums_ref[3:4, :] += column_sum(c)


def pack_pair(first, second):
    lane = lanes_of(first.shape[0])
    moved = pltpu.roll(second, DELTA, 1)
    return jnp.concatenate([jnp.where(lane < DELTA, first, moved), moved[:, :128]], axis=1).astype(BF)


def query_kernel(
    rel, idx, q_ref, pay_ref, k_ref, v_ref, n1_ref, da_ref, o_ref, dq_ref, gr_ref, sums_ref, full, low_o
):
    rows = pay_ref.shape[0] // 4
    heads = DELTA // DH
    lane = lanes_of(rows)
    sums_ref[...] = jnp.zeros_like(sums_ref)

    @pl.loop(0, 4)
    def _(i):
        here = pl.ds(pl.multiple_of(i * rows, rows), rows)
        pay = pay_ref[here, :]
        q = jnp.where(lane < DELTA, q_ref[here, :], pay)
        zero = jnp.zeros_like(q)
        dq = jnp.zeros((rows, LANES), F32)
        for h in range(heads):
            mask = head_lanes(lane, h)
            p = jnp.exp(nt(jnp.where(mask | piece_lanes(lane, LSE, h), q, zero), k_ref[...]))
            dp = nt(jnp.where(mask | piece_lanes(lane, DELTA, h), pay, zero), v_ref[...])
            dq = jnp.where(mask, nn((p * dp).astype(BF), k_ref[...]), dq)
        low = (dq * DH**-0.5).astype(BF)
        dq_ref[here, :] = low
        sums_ref[0:1, :] += column_sum(low.astype(F32))
        low_o[here, :] = o_ref[here, :].astype(BF)

    step = 128
    target = full if rel else gr_ref

    @pl.loop(0, n1_ref.shape[1] // step)
    def _(i):
        here = pl.ds(pl.multiple_of(i * step, step), step)
        target[here, :] = pack_pair(tn(n1_ref[:, here], dq_ref[...]), tn(da_ref[:, here], low_o[...]))

    if rel:
        place_blocks(full, gr_ref, idx, gr_ref.shape[2])


def key_kernel(
    rel, idx, k_ref, v_ref, q_ref, pay_ref, far_ref, n1_ref, dq_ref, w_ref, x_ref,
    gr_ref, dn_ref, sums_ref, col_ref, full, qall, pall, dkv,
):
    length = pay_ref.shape[0]
    rows = length // 4
    heads = DELTA // DH
    lane = lanes_of(rows)
    sums_ref[...] = jnp.zeros_like(sums_ref)
    col_ref[...] = jnp.zeros_like(col_ref)
    pall[:length, :] = pay_ref[...]
    for j in range(far_ref.shape[0]):
        pall[(j + 1) * length : (j + 2) * length, :] = far_ref[j]
    wide = lanes_of(length)
    for j in range(far_ref.shape[0] + 1):
        here = slice(j * length, (j + 1) * length)
        qall[here, :] = jnp.where(wide < DELTA, q_ref[here, :], pall[here, :])

    @pl.loop(0, 4)
    def _(i):
        here = pl.ds(pl.multiple_of(i * rows, rows), rows)
        k, v = k_ref[here, :], v_ref[here, :]
        zero, one = jnp.zeros_like(k), jnp.ones_like(k)
        dk = jnp.zeros((rows, LANES), F32)
        dv = jnp.zeros((rows, LANES), F32)
        for h in range(heads):
            mask = head_lanes(lane, h)
            left_k = jnp.where(mask, k, jnp.where(piece_lanes(lane, LSE, h), one, zero))
            left_v = jnp.where(mask, v, jnp.where(piece_lanes(lane, DELTA, h), one, zero))
            p = jnp.exp(nt(left_k, qall[...]))
            ds = (p * nt(left_v, pall[...])).astype(BF)
            dv = jnp.where(mask, nn(p.astype(BF), pall[...]), dv)
            dk = jnp.where(mask, nn(ds, qall[...]), dk)
        dk, dv, dq = dk.astype(BF), dv.astype(BF), dq_ref[here, :]
        col_ref[0:1, :] += column_sum(dv.astype(F32))
        every = jnp.concatenate([dq, dk, dv], axis=1)
        dkv[here, :] = every
        dn = nt(every, w_ref[...])
        put_halves(idx, i, rows, dn_ref, dn.astype(BF))
        xhat, _ = normalized(x_ref[here, :].astype(F32))
        sums_ref[0:1, :] += column_sum(dn * xhat)
        sums_ref[1:2, :] += column_sum(dn)

    step = 128
    target = full if rel else gr_ref

    @pl.loop(0, n1_ref.shape[1] // step)
    def _(i):
        here = pl.ds(pl.multiple_of(i * step, step), step)
        both = tn(n1_ref[:, here], dkv[:, LANES:])
        target[here, :] = pack_pair(both[:, :LANES], both[:, LANES:])

    if rel:
        place_blocks(full, gr_ref, idx, gr_ref.shape[2])


def last_kernel(idx, x_ref, a_ref, b_ref, dm_ref, vec_ref, out_ref):
    rows = x_ref.shape[0] // 4
    gain = vec_ref[0:1, :]

    @pl.loop(0, 4)
    def _(i):
        here = pl.ds(pl.multiple_of(i * rows, rows), rows)
        xhat, rstd = normalized(x_ref[here, :].astype(F32))
        dn = summed(idx, i, rows, a_ref, b_ref)
        out_ref[here, :] = (dm_ref[here, :] + norm_back(dn, gain, xhat, rstd)).astype(BF)


def out_kernel(idx, m_ref, a_ref, b_ref, vec_ref, out_ref):
    rows = m_ref.shape[0] // 4
    outb = vec_ref[5:6, :]

    @pl.loop(0, 4)
    def _(i):
        here = pl.ds(pl.multiple_of(i * rows, rows), rows)
        out_ref[here, :] = (m_ref[here, :] + summed(idx, i, rows, a_ref, b_ref) + outb).astype(BF)


def body(
    frames, w_qkv, w_out, w_fc1, w_fc2, head_bias, hidden_bias, ln_gain, ln_bias, out_bias, cotangent
):
    n_f, n_c, n_t = lax.axis_size("fsdp"), lax.axis_size("ctx"), lax.axis_size("tp")
    _, length, width = frames.shape
    piece, local = w_qkv.shape[1], w_qkv.shape[2]
    blocks = n_f * n_c
    rel = piece % 16 == 0
    t = lax.axis_index("tp")
    idx = jnp.stack([lax.axis_index("fsdp"), lax.axis_index("ctx"), t & 1]).astype(jnp.int32)
    x, cot = frames[0], cotangent[0]

    out_t = w_out.T
    parts = [
        w_qkv[0], out_t[:, :DH], w_qkv[1], out_t[:, DH : 2 * DH], w_qkv[2], out_t[:, 2 * DH :],
    ]
    first = jnp.concatenate(parts, axis=1)
    small = jnp.concatenate(
        [ln_gain.reshape(-1), ln_bias.reshape(-1), out_bias.reshape(-1), hidden_bias[0], head_bias[0]]
    )
    small = jnp.pad(small, (0, width - small.size))[None]
    first = jnp.concatenate([first, small, jnp.zeros((15, width), BF)], axis=0)

    def gathered(shard):
        near = jnp.stack([shard] + [send(shard, "ctx", k) for k in range(1, n_c)])
        parts = [near] + [send(near, "fsdp", k) for k in range(1, n_f)]
        return arrange(parts, piece, idx)

    w_all, rows = gathered(first)
    rows = rows[:, 0, :].astype(F32)
    six = rows[:, : 6 * piece].reshape(blocks, 6, piece).transpose(1, 0, 2).reshape(6, width)
    hidb = rows[:, 6 * piece : 7 * piece].reshape(1, width)
    vec = jnp.concatenate([six, hidb, jnp.zeros_like(hidb)], axis=0)
    hb = rows[:, 7 * piece : 7 * piece + 2 * local // blocks].reshape(2, local)
    hb = jnp.pad(hb, ((0, 0), (0, LANES - local)))
    wo = jnp.concatenate([w_all[:, j * LANES + DELTA : (j + 1) * LANES] for j in range(3)], axis=1)
    wo = jnp.pad(wo, ((0, 0), (0, LANES - local)))

    quarter = lax.dynamic_slice_in_dim(x, t * (length // n_t), length // n_t, 0)
    far = jnp.stack([send(quarter, "ctx", k) for k in range(1, n_c)])
    far = lax.all_gather(far, "tp", axis=1, tiled=True).reshape((n_c - 1) * length, width)

    fc1, _ = gathered(w_fc1)
    fc2, _ = gathered(w_fc2.T)

    n1, q, k, v, o, aux, branch = call(
        attend_kernel,
        (
            shape(length, width), shape(n_c * length, LANES), shape(n_c * length, LANES),
            shape(n_c * length, LANES), shape(length, LANES, dtype=F32), shape(length, LANES),
            shape(2, length // 2, width),
        ),
        x, far, w_all, wo, vec, hb,
        idx=idx, flops=5 * 10**9,
    )
    a0, a1 = tp_sum(branch)
    m, n2, g, df, mlp, dn2 = call(
        feed_kernel,
        (
            shape(length, width, dtype=F32), shape(length, width), shape(length, width),
            shape(length, width), shape(2, length // 2, width), shape(2, length // 2, width),
        ),
        x, a0, a1, cot, fc1, fc2, vec,
        idx=idx, flops=3 * 10**9,
    )
    b0, b1 = tp_sum(dn2)

    def grad_shape(cols):
        return shape(n_f, n_c, piece, cols) if rel else shape(width, cols)

    def as_blocks(grad):
        return grad if rel else relative(grad.reshape(n_f, n_c, piece, -1))

    gfc1, gfc2, hid = call(
        functools.partial(feed_grad_kernel, rel),
        (grad_shape(width), grad_shape(width), shape(1, width, dtype=F32)),
        n2, df, cot, g,
        scratch=[pltpu.VMEM((width, width), BF), pltpu.VMEM((width, width), BF)],
        idx=idx, flops=2 * 10**9,
    )
    dm, da, pay, sums2 = call(
        middle_kernel,
        (
            shape(length, width, dtype=F32), shape(length, width), shape(length, LANES),
            shape(8, width, dtype=F32),
        ),
        m, b0, b1, cot, o, aux, wo, vec,
        idx=idx, flops=2 * 10**8,
    )
    far_pay = jnp.stack([send(pay, "ctx", j) for j in range(1, n_c)])
    dq, gr_q, dq_sum = call(
        functools.partial(query_kernel, rel),
        (shape(length, LANES), grad_shape(2 * local), shape(8, LANES, dtype=F32)),
        q, pay, k, v, n1, da, o,
        scratch=[pltpu.VMEM((width, 2 * local), BF), pltpu.VMEM((length, LANES), BF)],
        idx=idx, flops=3 * 10**9,
    )
    total = n_c * length
    gr_kv, dn1, sums1, dv_sum = call(
        functools.partial(key_kernel, rel),
        (
            grad_shape(2 * local), shape(2, length // 2, width), shape(8, width, dtype=F32),
            shape(8, LANES, dtype=F32),
        ),
        k, v, q, pay, far_pay, n1, dq, w_all, x,
        scratch=[
            pltpu.VMEM((width, 2 * local), BF), pltpu.VMEM((total, LANES), BF),
            pltpu.VMEM((total, LANES), BF), pltpu.VMEM((length, 3 * LANES), BF),
        ],
        idx=idx, flops=5 * 10**9,
    )
    e0, e1 = tp_sum(dn1)
    input_grad = call(
        last_kernel, (shape(length, width),), x, e0, e1, dm, vec, idx=idx
    )[0]
    y0, y1 = tp_sum(mlp)
    output = call(out_kernel, (shape(length, width),), m, y0, y1, vec, idx=idx)[0]

    sum_one = sums1[:2]
    bit = 1
    while bit < n_t:
        sum_one = sum_one + flip(sum_one, "tp", bit)
        bit *= 2
    six = jnp.concatenate([sum_one[0:1], sums2[0:1], sum_one[1:2], sums2[1:4], hid], axis=0)
    six = six.reshape(7, blocks, piece).transpose(1, 0, 2).reshape(blocks, 7 * piece)
    heads = jnp.concatenate([dq_sum[0, :local], dv_sum[0, :local]]).reshape(blocks, 2 * local // blocks)
    little = jnp.concatenate([six, heads], axis=1)
    little = jnp.pad(little, ((0, 0), (0, width - little.shape[1]))).astype(BF)
    little = reduce_blocks(relative(little.reshape(n_f, n_c, 1, width)))[0]

    grad_fc1 = reduce_blocks(as_blocks(gfc1))
    grad_fc2 = reduce_blocks(as_blocks(gfc2)).T
    first_two = reduce_blocks(as_blocks(gr_q))
    last_two = reduce_blocks(as_blocks(gr_kv))
    grad_qkv = jnp.stack([first_two[:, :local], last_two[:, :local], last_two[:, local:]])
    grad_out = first_two[:, local:].T
    pairs = little[: 6 * piece].reshape(3, 2, piece)
    grad_hidden = little[6 * piece : 7 * piece][None]
    grad_head = little[7 * piece : 7 * piece + 2 * local // blocks][None]
    return (
        output[None], input_grad[None], grad_qkv, grad_out, grad_fc1, grad_fc2,
        grad_head, grad_hidden, pairs[0], pairs[1], pairs[2],
    )


def solution(mesh):
    shards = ("fsdp", "ctx")
    rows = P("fsdp", "ctx", None)
    qkv = P(None, shards, "tp")
    by_tp = P("tp", shards)
    norm = P(None, shards)
    weights = (qkv, by_tp, P(shards, "tp"), by_tp, by_tp, by_tp, norm, norm, norm)
    return jax.shard_map(
        body,
        mesh=mesh,
        in_specs=(rows, *weights, rows),
        out_specs=(rows, rows, *weights),
        check_vma=False,
    )
```

```python
import functools

import jax
import jax.numpy as jnp
import numpy as np
from jax import lax
from jax.experimental import pallas as pl
from jax.experimental.pallas import tpu as pltpu
from jax.sharding import PartitionSpec as P

DH = 64
EPS = 1e-05
BF = jnp.bfloat16
F32 = jnp.float32
LANES = 256
DELTA = 192
LSE = 224
PIECES = 3
VMEM_LIMIT = 56 * 1024 * 1024


def ring(axis, k):
    n = lax.axis_size(axis)
    return [(i, (i + k) % n) for i in range(n)]


def send(x, axis, k):
    return lax.ppermute(x, axis, ring(axis, k))


def flip(x, axis, bit):
    return lax.ppermute(x, axis, [(i, i ^ bit) for i in range(lax.axis_size(axis))])


def after(x, *others):
    return lax.optimization_barrier((x, others))[0]


def add_low(a, b):
    return (a.astype(F32) + b.astype(F32)).astype(BF)


def tp_half(both):
    return add_low(both[0], flip(both[1], "tp", 1))


def tp_rest(half, wait=()):
    bit = 2
    while bit < lax.axis_size("tp"):
        half = add_low(half, after(flip(half, "tp", bit), wait))
        bit *= 2
    return half, flip(half, "tp", 1)


def sums_over(x, axis):
    bit = 1
    while bit < lax.axis_size(axis):
        x = x + flip(x, axis, bit)
        bit *= 2
    return x


def turned(x, shift, axis):
    n = x.shape[axis]
    return jnp.take(x, (shift - jnp.arange(n)) % n, axis=axis)


def canonical(blocks):
    return turned(turned(blocks, lax.axis_index("fsdp"), 0), lax.axis_index("ctx"), 1)


def relative(blocks):
    f, c = lax.axis_index("fsdp"), lax.axis_index("ctx")
    blocks = jnp.take(blocks, (f + jnp.arange(blocks.shape[0])) % blocks.shape[0], axis=0)
    return jnp.take(blocks, (c + jnp.arange(blocks.shape[1])) % blocks.shape[1], axis=1)


def dot(a, b, da, db):
    return lax.dot_general(a, b, (((da,), (db,)), ((), ())), preferred_element_type=F32)


def nn(a, b):
    return dot(a, b, 1, 0)


def nt(a, b):
    return dot(a, b, 1, 1)


def tn(a, b):
    return dot(a, b, 0, 0)


def lanes_of(rows):
    return lax.broadcasted_iota(jnp.int32, (rows, LANES), 1)


def head_lanes(lane, h):
    return (lane >= h * DH) & (lane < (h + 1) * DH)


def piece_lanes(lane, first, h):
    return (lane >= first + PIECES * h) & (lane < first + PIECES * (h + 1))


def in_pieces(lane, first, h, column):
    out = jnp.zeros(lane.shape, F32)
    rest = column
    for j in range(PIECES):
        piece = rest.astype(BF).astype(F32)
        out = jnp.where(lane == first + PIECES * h + j, piece, out)
        rest = rest - piece
    return out


def normalized(x):
    mean = jnp.mean(x, axis=-1, keepdims=True)
    centered = x - mean
    var = jnp.mean(centered * centered, axis=-1, keepdims=True)
    rstd = lax.rsqrt(var + EPS)
    return centered * rstd, rstd


def norm_back(grad, gain, xhat, rstd):
    dx = grad * gain
    return rstd * (
        dx
        - jnp.mean(dx, axis=-1, keepdims=True)
        - xhat * jnp.mean(dx * xhat, axis=-1, keepdims=True)
    )


def column_sum(x):
    return jnp.sum(x, axis=0, keepdims=True)


def call(kernel, outs, *args, scratch=(), flops=0, idx=None):
    ins = [pl.BlockSpec(memory_space=pltpu.VMEM) for _ in args]
    if idx is not None:
        ins = [pl.BlockSpec(memory_space=pltpu.SMEM)] + ins
        args = (idx, *args)
    moved = sum(a.size * a.dtype.itemsize for a in args)
    moved += sum(o.size * o.dtype.itemsize for o in outs)
    return pl.pallas_call(
        kernel,
        out_shape=tuple(outs),
        in_specs=ins,
        out_specs=tuple(pl.BlockSpec(memory_space=pltpu.VMEM) for _ in outs),
        scratch_shapes=list(scratch),
        compiler_params=pltpu.CompilerParams(vmem_limit_bytes=VMEM_LIMIT),
        cost_estimate=pl.CostEstimate(flops=flops, bytes_accessed=moved, transcendentals=0),
    )(*args)


def shape(*dims, dtype=BF):
    return jax.ShapeDtypeStruct(dims, dtype)


def listed(groups):
    out = []
    for refs in groups:
        blocks = []
        for ref in refs:
            blocks += [ref.at[j] for j in range(ref.shape[0])] if len(ref.shape) == 3 else [ref]
        out.append(blocks)
    return out


def unpack(idx, groups, out_ref):
    f, c = idx[0], idx[1]
    groups = listed(groups)
    n_f, n_c, rows = len(groups), len(groups[0]), groups[0][0].shape[0]
    for a in range(n_f):
        for b in range(n_c):
            at = lax.rem(f - a + n_f, n_f) * n_c + lax.rem(c - b + n_c, n_c)
            out_ref[pl.ds(pl.multiple_of(at * rows, rows), rows), :] = groups[a][b][...]


def pack(idx, full_ref, refs):
    f, c = idx[0], idx[1]
    n_f, (n_c, rows, _) = len(refs), refs[0].shape
    for a in range(n_f):
        for b in range(n_c):
            at = lax.rem(f + a, n_f) * n_c + lax.rem(c + b, n_c)
            refs[a][b] = full_ref[pl.ds(pl.multiple_of(at * rows, rows), rows), :]


def split(refs, sizes):
    out = []
    for size in sizes:
        out.append(refs[:size])
        refs = refs[size:]
    return out, refs


def project(n1_ref, w_ref, hb, q_ref, k_ref, v_ref, at):
    rows, width = n1_ref.shape
    lane = lanes_of(rows)
    here = slice(at, at + rows)
    n1 = n1_ref[...]
    q = ((nn(n1, w_ref[:, :LANES]) + hb[:, :LANES]).astype(BF)) * jnp.asarray(DH**-0.5, BF)
    q_ref[here, :] = jnp.where(lane < DELTA, q, jnp.zeros_like(q))
    k = nn(n1, w_ref[:, LANES : 2 * LANES]).astype(BF)
    k_ref[here, :] = jnp.where(lane < DELTA, k, jnp.ones_like(k))
    v = (nn(n1, w_ref[:, 2 * LANES : width]) + hb[:, LANES:]).astype(BF)
    v_ref[here, :] = jnp.where(lane < DELTA, v, jnp.ones_like(v))


def norm_rows(x_ref, gain, shift, out_ref, rows):
    @pl.loop(0, x_ref.shape[0] // rows)
    def _(i):
        here = pl.ds(pl.multiple_of(i * rows, rows), rows)
        xhat, _ = normalized(x_ref[here, :].astype(F32))
        out_ref[here, :] = (xhat * gain + shift).astype(BF)


def first_kernel(w_ref, out_ref, cols_ref, first_ref):
    local = w_ref.shape[2]
    third = local // 3
    at = lax.broadcasted_iota(jnp.int32, (local, LANES), 0)
    lane = lax.broadcasted_iota(jnp.int32, (local, LANES), 1)
    keep = jnp.where(at == lane, 1.0, 0.0).astype(BF)
    for j in range(3):
        move = jnp.where((lane >= local) & (at == lane - local + j * third), 1.0, 0.0).astype(BF)
        first_ref[:, j * LANES : (j + 1) * LANES] = (nn(w_ref[j], keep) + tn(out_ref[...], move)).astype(BF)
    at = lax.broadcasted_iota(jnp.int32, (8, 128), 0)
    lane = lax.broadcasted_iota(jnp.int32, (8, 128), 1)
    first_ref[:, 3 * LANES :] = tn(cols_ref[...], jnp.where(at == lane, 1.0, 0.0).astype(BF)).astype(BF)


def own_kernel(sizes, idx, *refs):
    groups, refs = split(refs, sizes)
    x_ref, place_ref, w_ref, wo_ref, vec_ref, n1_ref, q_ref, k_ref, v_ref = refs
    unpack(idx, groups, w_ref)
    length, width = x_ref.shape
    heads = DELTA // DH
    step = 128
    lane = lanes_of(step)
    vec = jnp.transpose(w_ref[:, width:].astype(F32))[:8, :]
    vec_ref[...] = vec
    hb = nn(vec.astype(BF), place_ref[...])[7:8, :]
    norm_rows(x_ref, vec[0:1, :], vec[2:3, :], n1_ref, length // 4)
    project(n1_ref, w_ref, hb, q_ref, k_ref, v_ref, 0)

    @pl.loop(0, width // step)
    def _(i):
        here = pl.ds(pl.multiple_of(i * step, step), step)
        out = jnp.zeros((step, LANES), F32)
        for h in range(heads):
            group = w_ref[here, h * LANES : (h + 1) * LANES].astype(F32)
            out = jnp.where(head_lanes(lane, h), pltpu.roll(group, (h + 1) * DH, 1), out)
        wo_ref[here, :] = out.astype(BF)


def attend_kernel(masks, sizes, idx, *refs):
    groups, refs = split(refs, sizes)
    groups = listed(groups)
    w_ref, wo_ref, vec_ref, place_ref, qo_ref, ko_ref, vo_ref = refs[:7]
    q_ref, k_ref, v_ref, o_ref, aux_ref, mine_ref, other_ref, x_scr, n_scr, s_scr, acc = refs[7:]
    length = qo_ref.shape[0]
    total = k_ref.shape[0]
    heads = DELTA // DH
    vec = vec_ref[...]
    hb = nn(vec.astype(BF), place_ref[...])[7:8, :]
    q_ref[:length, :] = qo_ref[...]
    k_ref[:length, :] = ko_ref[...]
    v_ref[:length, :] = vo_ref[...]
    piece = groups[0][0].shape[0]
    for j in range(len(groups[0])):
        for mask, group in zip(masks, groups):
            at = lax.bitwise_xor(idx[3], mask) * piece
            x_scr[pl.ds(pl.multiple_of(at, piece), piece), :] = group[j][...]
        norm_rows(x_scr, vec[0:1, :], vec[2:3, :], n_scr, length // 4)
        project(n_scr, w_ref, hb, q_ref, k_ref, v_ref, (j + 1) * length)

    lane = lanes_of(length)
    chunk = total // 4
    o_ref[...] = jnp.zeros_like(o_ref)
    aux_ref[...] = jnp.zeros_like(aux_ref)
    for h in range(heads):
        mask = head_lanes(lane, h)
        q = jnp.where(mask, qo_ref[...], jnp.zeros((length, LANES), BF))
        top = jnp.full((length, 128), -jnp.inf, F32)
        for j in range(4):
            here = slice(j * chunk, (j + 1) * chunk)
            s = nt(q, k_ref[here, :])
            s_scr[:, here] = s
            for i in range(chunk // 128):
                top = jnp.maximum(top, s[:, i * 128 : (i + 1) * 128])
        top = jnp.max(top, axis=-1, keepdims=True)
        for j in range(4):
            here = slice(j * chunk, (j + 1) * chunk)
            part = nn(jnp.exp(s_scr[:, here] - top).astype(BF), v_ref[here, :])
            if j == 0:
                acc[...] = part
            else:
                acc[...] += part
        ev = acc[...]
        mass = ev[:, DELTA : DELTA + 1]
        o_ref[...] = jnp.where(mask, ev / mass, o_ref[...])
        aux_ref[...] += in_pieces(lane, LSE, h, -(top + jnp.log(mass))).astype(BF)
    rows = length // 2
    put_halves(idx, 0, mine_ref, other_ref, nt(o_ref[:rows, :].astype(BF), wo_ref[...]).astype(BF))
    put_halves(idx, 1, mine_ref, other_ref, nt(o_ref[rows:, :].astype(BF), wo_ref[...]).astype(BF))


def summed(idx, i, mine_ref, other_ref):
    return jnp.where(i == idx[2], mine_ref[...].astype(F32), other_ref[...].astype(F32))


def put_halves(idx, i, mine_ref, other_ref, value):
    @pl.when(i == idx[2])
    def _():
        mine_ref[...] = value

    @pl.when(i != idx[2])
    def _():
        other_ref[...] = value


def feed_kernel(sizes, idx, *refs):
    groups, refs = split(refs, sizes)
    x_ref, a_ref, b_ref, c_ref, vec_ref = refs[:5]
    m_ref, n2_ref, g_ref, df_ref, mlp0, mlp1, dn0, dn1, w1_ref, w2_ref = refs[5:]
    unpack(idx, groups[: len(groups) // 2], w1_ref)
    unpack(idx, groups[len(groups) // 2 :], w2_ref)
    rows = x_ref.shape[0] // 2
    gain, shift, outb, hidb = vec_ref[1:2, :], vec_ref[3:4, :], vec_ref[4:5, :], vec_ref[6:7, :]

    @pl.loop(0, 2)
    def _(i):
        here = pl.ds(pl.multiple_of(i * rows, rows), rows)
        m = x_ref[here, :].astype(F32) + (summed(idx, i, a_ref, b_ref) + outb)
        m_ref[here, :] = m
        xhat, _ = normalized(m)
        n2 = (xhat * gain + shift).astype(BF)
        n2_ref[here, :] = n2
        f = nn(n2, w1_ref[...]) + hidb
        cdf = 0.5 * (1.0 + lax.erf(f * (0.5**0.5)))
        g = (f * cdf).astype(BF)
        g_ref[here, :] = g
        dg = nn(c_ref[here, :], w2_ref[...])
        slope = cdf + f * (jnp.exp(-0.5 * f * f) * 0.3989422804014327)
        df = (dg * slope).astype(BF)
        df_ref[here, :] = df
        put_halves(idx, i, dn0, dn1, nt(df, w1_ref[...]).astype(BF))
        put_halves(idx, i, mlp0, mlp1, nt(g, w2_ref[...]).astype(BF))


def feed_grad_kernel(idx, n2_ref, df_ref, c_ref, g_ref, *refs):
    outs, (hid_ref, full1, full2) = refs[:-3], refs[-3:]
    hid_ref[...] = column_sum(df_ref[...].astype(F32))
    step = n2_ref.shape[1] // 2

    @pl.loop(0, 2)
    def _(i):
        here = pl.ds(pl.multiple_of(i * step, step), step)
        full1[here, :] = tn(n2_ref[:, here], df_ref[...]).astype(BF)
        full2[here, :] = tn(c_ref[:, here], g_ref[...]).astype(BF)

    pack(idx, full1, outs[: len(outs) // 2])
    pack(idx, full2, outs[len(outs) // 2 :])


def middle_kernel(
    idx, m_ref, a_ref, b_ref, c_ref, o_ref, aux_ref, wo_ref, vec_ref,
    dm_ref, da_ref, pay_ref, sums_ref,
):
    rows = m_ref.shape[0] // 2
    heads = DELTA // DH
    gain = vec_ref[1:2, :]
    lane = lanes_of(rows)
    sums_ref[...] = jnp.zeros_like(sums_ref)

    @pl.loop(0, 2)
    def _(i):
        here = pl.ds(pl.multiple_of(i * rows, rows), rows)
        xhat, rstd = normalized(m_ref[here, :])
        dn = summed(idx, i, a_ref, b_ref)
        c = c_ref[here, :].astype(F32)
        dm = c + norm_back(dn, gain, xhat, rstd)
        dm_ref[here, :] = dm
        da = dm.astype(BF)
        da_ref[here, :] = da
        do = nn(da, wo_ref[...]).astype(BF)
        prod = do.astype(F32) * o_ref[here, :]
        extra = aux_ref[here, :].astype(F32)
        for h in range(heads):
            delta = jnp.sum(jnp.where(head_lanes(lane, h), prod, 0.0), axis=-1, keepdims=True)
            extra = extra + in_pieces(lane, DELTA, h, -delta)
        pay_ref[here, :] = jnp.where(lane < DELTA, do, extra.astype(BF))
        sums_ref[0:1, :] += column_sum(dn * xhat)
        sums_ref[1:2, :] += column_sum(dn)
        sums_ref[2:3, :] += column_sum(da.astype(F32))
        sums_ref[3:4, :] += column_sum(c)


def pack_pair(first, second):
    lane = lanes_of(first.shape[0])
    moved = pltpu.roll(second, DELTA, 1)
    return jnp.concatenate([jnp.where(lane < DELTA, first, moved), moved[:, :128]], axis=1).astype(BF)


def query_kernel(idx, q_ref, pay_ref, k_ref, v_ref, n1_ref, da_ref, o_ref, *refs):
    outs, (dq_ref, sums_ref, full, acc) = refs[:-4], refs[-4:]
    length, width = n1_ref.shape
    total = k_ref.shape[0]
    heads = DELTA // DH
    lane = lanes_of(length)
    chunk = total // 4
    pay = pay_ref[...]
    q = jnp.where(lane < DELTA, q_ref[...], pay)
    zero = jnp.zeros_like(q)
    for h in range(heads):
        mask = head_lanes(lane, h)
        left_q = jnp.where(mask | piece_lanes(lane, LSE, h), q, zero)
        left_p = jnp.where(mask | piece_lanes(lane, DELTA, h), pay, zero)
        for j in range(4):
            here = slice(j * chunk, (j + 1) * chunk)
            p = jnp.exp(nt(left_q, k_ref[here, :]))
            ds = (p * nt(left_p, v_ref[here, :])).astype(BF)
            part = nn(ds, k_ref[here, :])
            if j == 0:
                acc[h] = part
            else:
                acc[h] += part
    dq = jnp.zeros((length, LANES), F32)
    for h in range(heads):
        dq = jnp.where(head_lanes(lane, h), acc[h], dq)
    low = (dq * DH**-0.5).astype(BF)
    dq_ref[...] = low
    sums_ref[...] = jnp.broadcast_to(column_sum(low.astype(F32)), sums_ref.shape)
    step = width // 2
    low_o = o_ref[...].astype(BF)

    for i in range(2):
        here = slice(i * step, (i + 1) * step)
        full[here, :] = pack_pair(tn(n1_ref[:, here], low), tn(da_ref[:, here], low_o))

    pack(idx, full, outs)


def key_kernel(n_far, *refs):
    far_refs, refs = refs[:n_far], refs[n_far:]
    k_ref, v_ref, q_ref, pay_ref, dq_ref, dkv_ref, qall, pall, acc_k, acc_v = refs
    length = pay_ref.shape[0]
    heads = DELTA // DH
    pall[:length, :] = pay_ref[...]
    for j, ref in enumerate(far_refs):
        pall[(j + 1) * length : (j + 2) * length, :] = ref[...]
    lane = lanes_of(length)
    for j in range(n_far + 1):
        here = slice(j * length, (j + 1) * length)
        qall[here, :] = jnp.where(lane < DELTA, q_ref[here, :], pall[here, :])
    chunk = qall.shape[0] // 4
    k, v = k_ref[...], v_ref[...]
    zero, one = jnp.zeros_like(k), jnp.ones_like(k)
    for h in range(heads):
        mask = head_lanes(lane, h)
        left_k = jnp.where(mask, k, jnp.where(piece_lanes(lane, LSE, h), one, zero))
        left_v = jnp.where(mask, v, jnp.where(piece_lanes(lane, DELTA, h), one, zero))
        for j in range(4):
            here = slice(j * chunk, (j + 1) * chunk)
            p = jnp.exp(nt(left_k, qall[here, :]))
            ds = (p * nt(left_v, pall[here, :])).astype(BF)
            part_v = nn(p.astype(BF), pall[here, :])
            part_k = nn(ds, qall[here, :])
            if j == 0:
                acc_v[h] = part_v
                acc_k[h] = part_k
            else:
                acc_v[h] += part_v
                acc_k[h] += part_k
    dk = jnp.zeros((length, LANES), F32)
    dv = jnp.zeros((length, LANES), F32)
    for h in range(heads):
        dk = jnp.where(head_lanes(lane, h), acc_k[h], dk)
        dv = jnp.where(head_lanes(lane, h), acc_v[h], dv)
    dkv_ref[:, :LANES] = dq_ref[...]
    dkv_ref[:, LANES : 2 * LANES] = dk.astype(BF)
    dkv_ref[:, 2 * LANES :] = dv.astype(BF)


def key_grad_kernel(idx, dkv_ref, n1_ref, w_ref, x_ref, sums2_ref, hid_ref, dqs_ref, place_ref, *refs):
    outs, (dn0, dn1, sums_ref, full, little) = refs[:-5], refs[-5:]
    length, width = x_ref.shape
    rows = length // 2
    sums_ref[...] = jnp.zeros_like(sums_ref)
    little[...] = jnp.zeros_like(little)

    @pl.loop(0, 2)
    def _(i):
        here = pl.ds(pl.multiple_of(i * rows, rows), rows)
        dn = nt(dkv_ref[here, :], w_ref[:, :width])
        put_halves(idx, i, dn0, dn1, dn.astype(BF))
        xhat, _ = normalized(x_ref[here, :].astype(F32))
        sums_ref[0:1, :] += column_sum(dn * xhat)
        sums_ref[2:3, :] += column_sum(dn)

    little[1:2, :] = sums2_ref[0:1, :]
    little[3:6, :] = sums2_ref[1:4, :]
    little[6:7, :] = hid_ref[...]
    col = column_sum(dkv_ref[:, 2 * LANES :].astype(F32))
    heads_row = jnp.concatenate([dqs_ref[0:1, :], col], axis=1)
    row = lax.broadcasted_iota(jnp.int32, (128, 2 * LANES), 0)
    heads_row = jnp.where(row == 7, heads_row, 0.0).astype(BF)
    full[:, 2 * DELTA :] = (jnp.transpose(little[...]) + nt(place_ref[...], heads_row)).astype(BF)
    step = width // 2
    for i in range(2):
        here = slice(i * step, (i + 1) * step)
        n1 = n1_ref[:, here]
        full[here, : 2 * DELTA] = pack_pair(tn(n1, dkv_ref[:, LANES : 2 * LANES]), tn(n1, dkv_ref[:, 2 * LANES :]))

    pack(idx, full, outs)


def add_kernel(sizes, with_norm, idx, *refs):
    groups, refs = split(refs, sizes)
    if with_norm:
        sums_ref, refs = refs[0], refs[1:]
        refs, pad, cols = refs[:-2], refs[-2], refs[-1]
        pad[...] = jnp.zeros_like(pad)
        pad[:8, :] = sums_ref[...]
        cols[...] = jnp.transpose(pad[...])
    f, c = idx[0], idx[1]
    n_c, rows = len(refs), refs[0].shape[0]
    for b in range(n_c):
        at = 0
        for group in groups:
            total = group[0][b].astype(F32)
            for ref in group[1:]:
                total = total + ref[b].astype(F32)
            wide = total.shape[1]
            if with_norm and group is groups[-1]:
                place = f * n_c + lax.rem(c + b, n_c)
                extra = cols[pl.ds(pl.multiple_of(place * rows, rows), rows), :]
                refs[b][:, at : at + wide - 128] = total[:, :-128].astype(BF)
                refs[b][:, at + wide - 128 : at + wide] = (total[:, -128:] + extra).astype(BF)
            else:
                refs[b][:, at : at + wide] = total.astype(BF)
            at += wide


def last_kernel(idx, x_ref, a_ref, b_ref, dm_ref, vec_ref, out_ref):
    rows = x_ref.shape[0] // 2
    gain = vec_ref[0:1, :]

    @pl.loop(0, 2)
    def _(i):
        here = pl.ds(pl.multiple_of(i * rows, rows), rows)
        xhat, rstd = normalized(x_ref[here, :].astype(F32))
        dn = summed(idx, i, a_ref, b_ref)
        out_ref[here, :] = (dm_ref[here, :] + norm_back(dn, gain, xhat, rstd)).astype(BF)


def out_kernel(idx, m_ref, a_ref, b_ref, vec_ref, out_ref):
    rows = m_ref.shape[0] // 2
    outb = vec_ref[5:6, :]

    @pl.loop(0, 2)
    def _(i):
        here = pl.ds(pl.multiple_of(i * rows, rows), rows)
        out_ref[here, :] = (m_ref[here, :] + summed(idx, i, a_ref, b_ref) + outb).astype(BF)


def total_kernel(local, each, *refs):
    ins, (qkv_ref, out_ref, head_ref, hid_ref, gain_ref, bias_ref, outb_ref) = refs[:-7], refs[-7:]
    total = ins[0][...].astype(F32)
    for ref in ins[1:]:
        total = total + ref[...].astype(F32)
    rows = total.shape[0]
    first, second = total[:, : 2 * local], total[:, 2 * local : 4 * local]
    qkv_ref[0] = first[:, :local]
    qkv_ref[1] = second[:, :local]
    qkv_ref[2] = pltpu.roll(second, local, 1)[:, :local]
    low = jnp.zeros((128 - rows, 2 * LANES), F32)
    mixed = jnp.concatenate([pltpu.roll(first, local, 1)[:, :LANES], total[:, 4 * local :], total[:, 4 * local :]], axis=1)
    flat = jnp.transpose(jnp.concatenate([mixed, low], axis=0))
    out_ref[...] = flat[:local, :rows]
    little = flat[LANES : LANES + 8, :rows]
    head_ref[...] = little[7:8, :each]
    hid_ref[...] = little[6:7, :]
    gain_ref[...] = little[0:2, :]
    bias_ref[...] = little[2:4, :]
    outb_ref[...] = little[4:6, :]


def body(
    frames, w_qkv, w_out, w_fc1, w_fc2, head_bias, hidden_bias, ln_gain, ln_bias, out_bias, cotangent
):
    n_f, n_c, n_t = lax.axis_size("fsdp"), lax.axis_size("ctx"), lax.axis_size("tp")
    _, length, width = frames.shape
    piece, local = w_qkv.shape[1], w_qkv.shape[2]
    blocks = n_f * n_c
    aligned = piece % 16 == 0
    f, t = lax.axis_index("fsdp"), lax.axis_index("tp")
    idx = jnp.stack([f, lax.axis_index("ctx"), t & 1, t]).astype(jnp.int32)
    x, cot = frames[0], cotangent[0]
    each = 2 * local // blocks
    place = np.zeros((width, 2 * LANES), np.float32)
    for b in range(blocks):
        for r in range(each):
            at = b * each + r
            place[b * piece + r, at % local + at // local * LANES] = 1
    place = jnp.asarray(place, BF)

    columns = jnp.concatenate(
        [ln_gain, ln_bias, out_bias, hidden_bias, jnp.pad(head_bias, ((0, 0), (0, piece - each)))], axis=0
    )
    (first,) = call(first_kernel, (shape(piece, width + 128),), w_qkv, w_out, columns, flops=10**9)

    def near_blocks(shard):
        return [shard] + [send(shard, "ctx", k) for k in range(1, n_c)]

    def ordered(groups):
        if aligned:
            return groups
        groups = [jnp.concatenate([b if b.ndim == 3 else b[None] for b in g]) for g in groups]
        groups = jnp.stack(groups)
        return [[canonical(groups).reshape(1, width, -1)]]

    near = near_blocks(first)
    rest = jnp.stack(near[1:])
    own_far = [send(first, "fsdp", a) for a in range(1, n_f)]
    quarter = lax.dynamic_slice_in_dim(x, t * (length // n_t), length // n_t, 0)
    quarter = after(quarter, near, own_far)
    rest_far = [send(after(rest, own_far), "fsdp", a) for a in range(1, n_f)]
    far = jnp.stack([send(quarter, "ctx", k) for k in range(1, n_c)])
    w_groups = ordered([near] + [[a, b] for a, b in zip(own_far, rest_far)])
    far = after(far, rest_far)
    quarters = {0: far}
    bit = n_t // 2
    while bit > 0:
        for mask in list(quarters):
            quarters[mask ^ bit] = flip(quarters[mask], "tp", bit)
        bit //= 2
    quarters = {mask: [q] for mask, q in quarters.items()}
    masks = tuple(quarters)

    def stacked_groups(near):
        return ordered([[near]] + [[send(near, "fsdp", a)] for a in range(1, n_f)])

    near1 = jnp.stack(near_blocks(after(w_fc1, far, rest_far)))
    fc1 = stacked_groups(near1)
    near2 = jnp.stack(near_blocks(after(w_fc2.T, near1, quarters)))
    fc2 = stacked_groups(near2)

    def sizes(groups):
        return tuple(len(g) for g in groups)

    def flat(groups):
        return [r for g in groups for r in g]

    halves = (shape(length // 2, width), shape(length // 2, width))
    rows_of = shape(length, LANES)
    w_all, wo, vec, n1, q_own, k_own, v_own = call(
        functools.partial(own_kernel, sizes(w_groups)),
        (
            shape(width, width + 128), shape(width, LANES), shape(8, width, dtype=F32),
            shape(length, width), rows_of, rows_of, rows_of,
        ),
        *flat(w_groups), x, place,
        idx=idx, flops=6 * 10**9,
    )
    total = n_c * length
    every = shape(total, LANES)
    q_groups = list(quarters.values())
    q, k, v, o, aux, *branch = call(
        functools.partial(attend_kernel, masks, sizes(q_groups)),
        (every, every, every, shape(length, LANES, dtype=F32), rows_of, *halves),
        *flat(q_groups), w_all, wo, vec, place, after(q_own, near1), k_own, v_own,
        scratch=[
            pltpu.VMEM((length, width), BF), pltpu.VMEM((length, width), BF),
            pltpu.VMEM((length, total), F32), pltpu.VMEM((length, LANES), F32),
        ],
        idx=idx, flops=14 * 10**9,
    )
    a0, a1 = tp_rest(tp_half((branch[0], after(branch[1], near2, fc1))))
    m, n2, g, df, mlp0, mlp1, dn0, dn1 = call(
        functools.partial(feed_kernel, sizes(fc1) + sizes(fc2)),
        (
            shape(length, width, dtype=F32), shape(length, width), shape(length, width),
            shape(length, width), *halves, *halves,
        ),
        *flat(fc1), *flat(fc2), x, a0, a1, cot, vec,
        scratch=[pltpu.VMEM((width, width), BF), pltpu.VMEM((width, width), BF)],
        idx=idx, flops=10 * 10**9,
    )
    dn_half = tp_half((dn0, dn1))

    def packed(cols):
        if aligned:
            return tuple(shape(n_c, piece, cols) for _ in range(n_f))
        return (shape(1, width, cols),)

    def as_blocks(parts):
        if aligned:
            return parts
        parts = relative(parts[0].reshape(n_f, n_c, piece, -1))
        return [parts[a] for a in range(n_f)]

    *gfc, hid = call(
        feed_grad_kernel,
        (*packed(width), *packed(width), shape(1, width, dtype=F32)),
        n2, after(df, dn_half), cot, g,
        scratch=[pltpu.VMEM((width, width), BF), pltpu.VMEM((width, width), BF)],
        idx=idx, flops=5 * 10**9,
    )
    b0, b1 = tp_rest(dn_half, hid)
    dm, da, pay, sums2 = call(
        middle_kernel,
        (
            shape(length, width, dtype=F32), shape(length, width), shape(length, LANES),
            shape(8, width, dtype=F32),
        ),
        m, b0, b1, cot, o, aux, wo, vec,
        idx=idx, flops=5 * 10**9,
    )
    far_pay = [send(pay, "ctx", j) for j in range(1, n_c)]

    def over_fsdp(parts):
        parts = as_blocks(parts)
        return [parts[0]] + [send(parts[a], "fsdp", a) for a in range(1, n_f)]

    def added(groups, wait, norm=None):
        groups = [[g[0], *after(g[1:], wait)] for g in groups]
        cols = sum(g[0].shape[-1] for g in groups)
        if not aligned:
            total = jnp.concatenate([sum(p.astype(F32) for p in g) for g in groups], axis=-1)
            if norm is not None:
                rows = relative(norm.T.reshape(n_f, n_c, piece, 8))[0]
                total = total.at[..., cols - 128 : cols - 120].add(rows)
            return list(total.astype(BF))
        extra = () if norm is None else (norm,)
        scratch = () if norm is None else (pltpu.VMEM((128, width), F32), pltpu.VMEM((width, 128), F32))
        return call(
            functools.partial(add_kernel, sizes(groups), norm is not None),
            tuple(shape(piece, cols) for _ in range(n_c)),
            *flat(groups), *extra,
            scratch=scratch, idx=idx, flops=10**9,
        )

    def over_ctx(low):
        return [low[0]] + [send(low[j], "ctx", j) for j in range(1, n_c)]

    def sum_of(parts):
        return sum(p.astype(F32) for p in parts)

    gfc1 = over_fsdp(gfc[: len(gfc) // 2])
    gfc2 = over_fsdp([after(p, gfc1) for p in gfc[len(gfc) // 2 :]])
    *gr_q, dq, dq_sum = call(
        query_kernel,
        (*packed(2 * local), rows_of, shape(8, LANES, dtype=F32)),
        q_own, after(pay, gfc1), k, v, n1, da, o,
        scratch=[pltpu.VMEM((width, 2 * local), BF), pltpu.VMEM((DELTA // DH, length, LANES), F32)],
        idx=idx, flops=10 * 10**9,
    )
    gfc1 = over_ctx(after(added([gfc1], dq), far_pay))
    gfc2_low = added([gfc2], far_pay)
    y0, y1 = tp_rest(tp_half((mlp0, after(mlp1, pay))))
    gr_q = over_fsdp(gr_q)
    (dkv,) = call(
        functools.partial(key_kernel, n_c - 1),
        (shape(length, 3 * LANES),),
        *far_pay, k_own, v_own, q, after(pay, gfc1[0], gfc2_low, y0), dq,
        scratch=[
            pltpu.VMEM((total, LANES), BF), pltpu.VMEM((total, LANES), BF),
            pltpu.VMEM((DELTA // DH, length, LANES), F32), pltpu.VMEM((DELTA // DH, length, LANES), F32),
        ],
        flops=12 * 10**9,
    )
    gfc2 = over_ctx(after(gfc2_low, dkv))
    *gr_kv, dx0, dx1, sums1 = call(
        key_grad_kernel,
        (*packed(2 * local + 128), *halves, shape(8, width, dtype=F32)),
        after(dkv, gfc1, gr_q), n1, w_all, x, sums2, hid, dq_sum, place,
        scratch=[pltpu.VMEM((width, 2 * local + 128), BF), pltpu.VMEM((128, width), F32)],
        idx=idx, flops=5 * 10**9,
    )
    e_half = tp_half((dx0, after(dx1, gfc2)))
    gr_kv = over_fsdp(gr_kv)
    sums1 = sums_over(after(sums_over(sums1, "tp"), gr_kv), "fsdp")
    rest = over_ctx(added([gr_q, gr_kv], sums1, sums1))
    output = call(
        out_kernel, (shape(length, width),), m, y0, y1, vec, idx=idx, flops=2 * 10**9
    )[0]
    e0, e1 = tp_rest(e_half)
    input_grad = call(
        last_kernel, (shape(length, width),), x, e0, e1, dm, vec, idx=idx, flops=3 * 10**9
    )[0]

    fc1_grad, fc2_grad = sum_of(gfc1), sum_of(gfc2).T
    if aligned:
        qkv_grad, out_grad, head, hidden, gain, bias, outb = call(
            functools.partial(total_kernel, local, each),
            tuple(
                shape(*dims, dtype=F32)
                for dims in (
                    (3, piece, local), (local, piece), (1, each), (1, piece), (2, piece), (2, piece), (2, piece),
                )
            ),
            *rest,
            flops=2 * 10**9,
        )
    else:
        sums = sum_of(rest)
        cuts = [sums[:, j * local : (j + 1) * local] for j in range(4)]
        little = sums[:, 4 * local : 4 * local + 8].T
        qkv_grad, out_grad = jnp.stack([cuts[0], cuts[2], cuts[3]]), cuts[1].T
        head, hidden = little[7:8, :each], little[6:7]
        gain, bias, outb = little[0:2], little[2:4], little[4:6]
    return (
        output[None], input_grad[None], qkv_grad, out_grad, fc1_grad, fc2_grad, head, hidden, gain, bias, outb,
    )


def solution(mesh):
    shards = ("fsdp", "ctx")
    rows = P("fsdp", "ctx", None)
    qkv = P(None, shards, "tp")
    by_tp = P("tp", shards)
    norm = P(None, shards)
    weights = (qkv, by_tp, P(shards, "tp"), by_tp, by_tp, by_tp, norm, norm, norm)
    return jax.shard_map(
        body,
        mesh=mesh,
        in_specs=(rows, *weights, rows),
        out_specs=(rows, rows, *weights),
        check_vma=False,
    )
```

```python
import functools

import jax
import jax.numpy as jnp
import numpy as np
from jax import lax
from jax.experimental import pallas as pl
from jax.experimental.pallas import tpu as pltpu
from jax.sharding import PartitionSpec as P

DH = 64
EPS = 1e-05
BF = jnp.bfloat16
F32 = jnp.float32
LANES = 256
DELTA = 192
LSE = 198
SENT = 208
VMEM_LIMIT = 20 * 1024 * 1024


def ring(axis, k):
    n = lax.axis_size(axis)
    return [(i, (i + k) % n) for i in range(n)]


def send(x, axis, k):
    return lax.ppermute(x, axis, ring(axis, k))


def flip(x, axis, bit):
    return lax.ppermute(x, axis, [(i, i ^ bit) for i in range(lax.axis_size(axis))])


def after(x, *others):
    return lax.optimization_barrier((x, others))[0]


def add_low(a, b):
    return (a.astype(F32) + b.astype(F32)).astype(BF)


def tp_half(both):
    return add_low(both[0], flip(both[1], "tp", 1))


def tp_rest(half, wait=()):
    bit = 2
    while bit < lax.axis_size("tp"):
        half = add_low(half, after(flip(half, "tp", bit), wait))
        bit *= 2
    return half, flip(half, "tp", 1)


def sums_over(x, axis):
    bit = 1
    while bit < lax.axis_size(axis):
        x = x + flip(x, axis, bit)
        bit *= 2
    return x


def turned(x, shift, axis):
    n = x.shape[axis]
    return jnp.take(x, (shift - jnp.arange(n)) % n, axis=axis)


def canonical(blocks):
    return turned(turned(blocks, lax.axis_index("fsdp"), 0), lax.axis_index("ctx"), 1)


def relative(blocks):
    f, c = lax.axis_index("fsdp"), lax.axis_index("ctx")
    blocks = jnp.take(blocks, (f + jnp.arange(blocks.shape[0])) % blocks.shape[0], axis=0)
    return jnp.take(blocks, (c + jnp.arange(blocks.shape[1])) % blocks.shape[1], axis=1)


def dot(a, b, da, db):
    return lax.dot_general(a, b, (((da,), (db,)), ((), ())), preferred_element_type=F32)


def nn(a, b):
    return dot(a, b, 1, 0)


def nt(a, b):
    return dot(a, b, 1, 1)


def tn(a, b):
    return dot(a, b, 0, 0)


def lanes_of(rows):
    return lax.broadcasted_iota(jnp.int32, (rows, LANES), 1)


def head_lanes(lane, h):
    return (lane >= h * DH) & (lane < (h + 1) * DH)


def piece_lanes(lane, first, h):
    count = 2 if first == DELTA else 3
    return (lane >= first + count * h) & (lane < first + count * (h + 1))


def in_pieces(lane, first, h, column):
    count = 2 if first == DELTA else 3
    out = jnp.zeros(lane.shape, F32)
    rest = column
    for j in range(count):
        piece = rest.astype(BF).astype(F32)
        out = jnp.where(lane == first + count * h + j, piece, out)
        rest = rest - piece
    return out


def chosen():
    row = lax.broadcasted_iota(jnp.int32, (SENT, LANES), 0)
    lane = lax.broadcasted_iota(jnp.int32, (SENT, LANES), 1)
    return jnp.where(row == lane, 1.0, 0.0).astype(BF)


def normalized(x):
    mean = jnp.mean(x, axis=-1, keepdims=True)
    centered = x - mean
    var = jnp.mean(centered * centered, axis=-1, keepdims=True)
    rstd = lax.rsqrt(var + EPS)
    return centered * rstd, rstd


def norm_back(grad, gain, xhat, rstd):
    dx = grad * gain
    return rstd * (
        dx
        - jnp.mean(dx, axis=-1, keepdims=True)
        - xhat * jnp.mean(dx * xhat, axis=-1, keepdims=True)
    )


def column_sum(x):
    return jnp.sum(x, axis=0, keepdims=True)


def call(kernel, outs, *args, scratch=(), flops=0, idx=None, where=pltpu.VMEM, limit=VMEM_LIMIT):
    ins = [pl.BlockSpec(memory_space=where) for _ in args]
    if idx is not None:
        ins = [pl.BlockSpec(memory_space=pltpu.SMEM)] + ins
        args = (idx, *args)
    moved = sum(a.size * a.dtype.itemsize for a in args)
    moved += sum(o.size * o.dtype.itemsize for o in outs)
    return pl.pallas_call(
        kernel,
        out_shape=tuple(outs),
        in_specs=ins,
        out_specs=tuple(pl.BlockSpec(memory_space=pltpu.VMEM) for _ in outs),
        scratch_shapes=list(scratch),
        compiler_params=pltpu.CompilerParams(vmem_limit_bytes=limit),
        cost_estimate=pl.CostEstimate(flops=flops, bytes_accessed=moved, transcendentals=0),
    )(*args)


def shape(*dims, dtype=BF):
    return jax.ShapeDtypeStruct(dims, dtype)


def listed(groups):
    out = []
    for refs in groups:
        blocks = []
        for ref in refs:
            blocks += [ref.at[j] for j in range(ref.shape[0])] if len(ref.shape) == 3 else [ref]
        out.append(blocks)
    return out


def unpack(idx, groups, out_ref):
    f, c = idx[0], idx[1]
    groups = listed(groups)
    n_f, n_c, rows = len(groups), len(groups[0]), groups[0][0].shape[0]
    for a in range(n_f):
        for b in range(n_c):
            at = lax.rem(f - a + n_f, n_f) * n_c + lax.rem(c - b + n_c, n_c)
            out_ref[pl.ds(pl.multiple_of(at * rows, rows), rows), :] = groups[a][b][...]


def pack(idx, full_ref, refs):
    f, c = idx[0], idx[1]
    n_f, (n_c, rows, _) = len(refs), refs[0].shape
    for a in range(n_f):
        for b in range(n_c):
            at = lax.rem(f + a, n_f) * n_c + lax.rem(c + b, n_c)
            refs[a][b] = full_ref[pl.ds(pl.multiple_of(at * rows, rows), rows), :]


def split(refs, sizes):
    out = []
    for size in sizes:
        out.append(refs[:size])
        refs = refs[size:]
    return out, refs


def project(n1_ref, w_ref, hb, q_ref, k_ref, v_ref, at):
    rows, width = n1_ref.shape
    lane = lanes_of(rows)
    here = slice(at, at + rows)
    n1 = n1_ref[...]
    q = ((nn(n1, w_ref[:, :LANES]) + hb[:, :LANES]).astype(BF)) * jnp.asarray(DH**-0.5, BF)
    q_ref[here, :] = jnp.where(lane < DELTA, q, jnp.zeros_like(q))
    k = nn(n1, w_ref[:, LANES : 2 * LANES]).astype(BF)
    k_ref[here, :] = jnp.where(lane < DELTA, k, jnp.ones_like(k))
    v = (nn(n1, w_ref[:, 2 * LANES : width]) + hb[:, LANES:]).astype(BF)
    v_ref[here, :] = jnp.where(lane < DELTA, v, jnp.ones_like(v))


def norm_rows(x_ref, gain, shift, out_ref, rows):
    @pl.loop(0, x_ref.shape[0] // rows)
    def _(i):
        here = pl.ds(pl.multiple_of(i * rows, rows), rows)
        xhat, _ = normalized(x_ref[here, :].astype(F32))
        out_ref[here, :] = (xhat * gain + shift).astype(BF)


def first_kernel(
    idx, w_any, out_any, gain_any, bias_any, outb_any, hid_any, head_any, x_any, first_ref, *refs
):
    packet_ref, (w_ref, out_ref, *vectors, x_ref, sems) = refs[:-9], refs[-9:]
    rows = x_ref.shape[0]
    pairs = [
        (w_any, w_ref), (out_any, out_ref), *zip((gain_any, bias_any, outb_any, hid_any, head_any), vectors),
        (x_any.at[pl.ds(pl.multiple_of(idx[3] * rows, rows), rows), :], x_ref),
    ]
    copies = [pltpu.make_async_copy(a, b, sems.at[k]) for k, (a, b) in enumerate(pairs)]
    for copy in copies:
        copy.start()
    for copy in copies:
        copy.wait()
    local = w_ref.shape[2]
    third = local // 3
    at = lax.broadcasted_iota(jnp.int32, (local, LANES), 0)
    lane = lax.broadcasted_iota(jnp.int32, (local, LANES), 1)
    keep = jnp.where(at == lane, 1.0, 0.0).astype(BF)
    for j in range(3):
        move = jnp.where((lane >= local) & (at == lane - local + j * third), 1.0, 0.0).astype(BF)
        first_ref[:, j * LANES : (j + 1) * LANES] = (nn(w_ref[j], keep) + tn(out_ref[...], move)).astype(BF)
    columns = jnp.zeros((first_ref.shape[0], 128), F32)
    begin = 0
    for ref in vectors:
        count, size = ref.shape
        vec = ref[...]
        if size < first_ref.shape[0]:
            row = lax.broadcasted_iota(jnp.int32, (size, first_ref.shape[0]), 0)
            col = lax.broadcasted_iota(jnp.int32, (size, first_ref.shape[0]), 1)
            vec = nn(vec, jnp.where(row == col, 1.0, 0.0).astype(BF)).astype(BF)
        at = lax.broadcasted_iota(jnp.int32, (count, 128), 0)
        lane = lax.broadcasted_iota(jnp.int32, (count, 128), 1)
        columns = columns + tn(vec, jnp.where(lane == at + begin, 1.0, 0.0).astype(BF))
        begin += count
    first_ref[:, 3 * LANES :] = columns.astype(BF)
    for ref in packet_ref:
        ref[:, : first_ref.shape[1]] = first_ref[...]
        ref[:, first_ref.shape[1] :] = x_ref[...]


def own_kernel(sizes, idx, *refs):
    groups, refs = split(refs, sizes)
    x_ref, place_ref, w_ref, wo_ref, vec_ref, n1_ref, q_ref, k_ref, v_ref = refs
    unpack(idx, groups, w_ref)
    length, width = x_ref.shape
    heads = DELTA // DH
    step = 128
    lane = lanes_of(step)
    vec = jnp.transpose(w_ref[:, width:].astype(F32))[:8, :]
    vec_ref[...] = vec
    hb = nn(vec.astype(BF), place_ref[...])[7:8, :]
    norm_rows(x_ref, vec[0:1, :], vec[2:3, :], n1_ref, length // 4)
    project(n1_ref, w_ref, hb, q_ref, k_ref, v_ref, 0)

    @pl.loop(0, width // step)
    def _(i):
        here = pl.ds(pl.multiple_of(i * step, step), step)
        out = jnp.zeros((step, LANES), F32)
        for h in range(heads):
            group = w_ref[here, h * LANES : (h + 1) * LANES].astype(F32)
            out = jnp.where(head_lanes(lane, h), pltpu.roll(group, (h + 1) * DH, 1), out)
        wo_ref[here, :] = out.astype(BF)


def attend_kernel(masks, sizes, idx, *refs):
    groups, refs = split(refs, sizes)
    groups = listed(groups)
    w_ref, wo_ref, vec_ref, place_ref, qo_ref, ko_ref, vo_ref = refs[:7]
    q_ref, k_ref, v_ref, o_ref, aux_ref, mine_ref, other_ref, x_scr, n_scr, s_scr, acc = refs[7:]
    length = qo_ref.shape[0]
    total = k_ref.shape[0]
    heads = DELTA // DH
    vec = vec_ref[...]
    hb = nn(vec.astype(BF), place_ref[...])[7:8, :]
    q_ref[:length, :] = qo_ref[...]
    k_ref[:length, :] = ko_ref[...]
    v_ref[:length, :] = vo_ref[...]
    piece = groups[0][0].shape[0]
    for j in range(len(groups[0])):
        for mask, group in zip(masks, groups):
            at = lax.bitwise_xor(idx[3], mask) * piece
            x_scr[pl.ds(pl.multiple_of(at, piece), piece), :] = group[j][...]
        norm_rows(x_scr, vec[0:1, :], vec[2:3, :], n_scr, length // 4)
        project(n_scr, w_ref, hb, q_ref, k_ref, v_ref, (j + 1) * length)

    lane = lanes_of(length)
    chunk = total // 4
    o_ref[...] = jnp.zeros_like(o_ref)
    aux_ref[...] = jnp.zeros_like(aux_ref)
    for h in range(heads):
        mask = head_lanes(lane, h)
        q = jnp.where(mask, qo_ref[...], jnp.zeros((length, LANES), BF))
        top = jnp.full((length, 128), -jnp.inf, F32)
        for j in range(4):
            here = slice(j * chunk, (j + 1) * chunk)
            s = nt(q, k_ref[here, :])
            s_scr[:, here] = s
            for i in range(chunk // 128):
                top = jnp.maximum(top, s[:, i * 128 : (i + 1) * 128])
        top = jnp.max(top, axis=-1, keepdims=True)
        for j in range(4):
            here = slice(j * chunk, (j + 1) * chunk)
            part = nn(jnp.exp(s_scr[:, here] - top).astype(BF), v_ref[here, :])
            if j == 0:
                acc[...] = part
            else:
                acc[...] += part
        ev = acc[...]
        mass = ev[:, DELTA : DELTA + 1]
        o_ref[...] = jnp.where(mask, ev / mass, o_ref[...])
        aux_ref[...] += in_pieces(lane, LSE, h, -(top + jnp.log(mass))).astype(BF)
    rows = length // 2
    put_halves(idx, 0, mine_ref, other_ref, nt(o_ref[:rows, :].astype(BF), wo_ref[...]).astype(BF))
    put_halves(idx, 1, mine_ref, other_ref, nt(o_ref[rows:, :].astype(BF), wo_ref[...]).astype(BF))


def summed(idx, i, mine_ref, other_ref):
    return jnp.where(i == idx[2], mine_ref[...].astype(F32), other_ref[...].astype(F32))


def put_halves(idx, i, mine_ref, other_ref, value):
    @pl.when(i == idx[2])
    def _():
        mine_ref[...] = value

    @pl.when(i != idx[2])
    def _():
        other_ref[...] = value


def feed_kernel(sizes, idx, *refs):
    groups, refs = split(refs, sizes)
    x_ref, a_ref, b_ref, c_ref, vec_ref = refs[:5]
    m_ref, n2_ref, g_ref, df_ref, mlp0, mlp1, dn0, dn1, w1_ref, w2_ref = refs[5:]
    unpack(idx, groups[: len(groups) // 2], w1_ref)
    unpack(idx, groups[len(groups) // 2 :], w2_ref)
    rows = x_ref.shape[0] // 2
    gain, shift, outb, hidb = vec_ref[1:2, :], vec_ref[3:4, :], vec_ref[4:5, :], vec_ref[6:7, :]

    @pl.loop(0, 2)
    def _(i):
        here = pl.ds(pl.multiple_of(i * rows, rows), rows)
        m = x_ref[here, :].astype(F32) + (summed(idx, i, a_ref, b_ref) + outb)
        m_ref[here, :] = m
        xhat, _ = normalized(m)
        n2 = (xhat * gain + shift).astype(BF)
        n2_ref[here, :] = n2
        f = nn(n2, w1_ref[...]) + hidb
        cdf = 0.5 * (1.0 + lax.erf(f * (0.5**0.5)))
        g = (f * cdf).astype(BF)
        g_ref[here, :] = g
        dg = nn(c_ref[here, :], w2_ref[...])
        slope = cdf + f * (jnp.exp(-0.5 * f * f) * 0.3989422804014327)
        df = (dg * slope).astype(BF)
        df_ref[here, :] = df
        put_halves(idx, i, dn0, dn1, nt(df, w1_ref[...]).astype(BF))
        put_halves(idx, i, mlp0, mlp1, nt(g, w2_ref[...]).astype(BF))


def feed_grad_kernel(idx, n2_ref, df_ref, c_ref, g_ref, *refs):
    outs, (hid_ref, full1, full2) = refs[:-3], refs[-3:]
    hid_ref[...] = column_sum(df_ref[...].astype(F32))
    step = n2_ref.shape[1] // 2

    @pl.loop(0, 2)
    def _(i):
        here = pl.ds(pl.multiple_of(i * step, step), step)
        full1[here, :] = tn(n2_ref[:, here], df_ref[...]).astype(BF)
        full2[here, :] = tn(c_ref[:, here], g_ref[...]).astype(BF)

    pack(idx, full1, outs[: len(outs) // 2])
    pack(idx, full2, outs[len(outs) // 2 :])


def middle_kernel(
    idx, m_ref, a_ref, b_ref, c_ref, o_ref, aux_ref, wo_ref, vec_ref,
    dm_ref, da_ref, pay_ref, sent_ref, sums_ref,
):
    rows = m_ref.shape[0] // 2
    heads = DELTA // DH
    gain = vec_ref[1:2, :]
    lane = lanes_of(rows)
    sums_ref[...] = jnp.zeros_like(sums_ref)

    @pl.loop(0, 2)
    def _(i):
        here = pl.ds(pl.multiple_of(i * rows, rows), rows)
        xhat, rstd = normalized(m_ref[here, :])
        dn = summed(idx, i, a_ref, b_ref)
        c = c_ref[here, :].astype(F32)
        dm = c + norm_back(dn, gain, xhat, rstd)
        dm_ref[here, :] = dm
        da = dm.astype(BF)
        da_ref[here, :] = da
        do = nn(da, wo_ref[...]).astype(BF)
        prod = do.astype(F32) * o_ref[here, :]
        extra = aux_ref[here, :].astype(F32)
        for h in range(heads):
            delta = jnp.sum(jnp.where(head_lanes(lane, h), prod, 0.0), axis=-1, keepdims=True)
            extra = extra + in_pieces(lane, DELTA, h, -delta)
        pay_ref[here, :] = jnp.where(lane < DELTA, do, extra.astype(BF))
        sums_ref[0:1, :] += column_sum(dn * xhat)
        sums_ref[1:2, :] += column_sum(dn)
        sums_ref[2:3, :] += column_sum(da.astype(F32))
        sums_ref[3:4, :] += column_sum(c)

    sent_ref[...] = nt(chosen(), pay_ref[...]).astype(BF)


def pack_pair(first, second):
    lane = lanes_of(first.shape[0])
    moved = pltpu.roll(second, DELTA, 1)
    return jnp.concatenate([jnp.where(lane < DELTA, first, moved), moved[:, :128]], axis=1).astype(BF)


def query_kernel(idx, q_ref, pay_ref, k_ref, v_ref, n1_ref, da_ref, o_ref, *refs):
    outs, (dq_ref, sums_ref, full, acc) = refs[:-4], refs[-4:]
    length, width = n1_ref.shape
    total = k_ref.shape[0]
    heads = DELTA // DH
    lane = lanes_of(length)
    chunk = total // 4
    pay = pay_ref[...]
    q = jnp.where(lane < DELTA, q_ref[...], pay)
    zero = jnp.zeros_like(q)
    for h in range(heads):
        mask = head_lanes(lane, h)
        left_q = jnp.where(mask | piece_lanes(lane, LSE, h), q, zero)
        left_p = jnp.where(mask | piece_lanes(lane, DELTA, h), pay, zero)
        for j in range(4):
            here = slice(j * chunk, (j + 1) * chunk)
            p = jnp.exp(nt(left_q, k_ref[here, :]))
            ds = (p * nt(left_p, v_ref[here, :])).astype(BF)
            part = nn(ds, k_ref[here, :])
            if j == 0:
                acc[h] = part
            else:
                acc[h] += part
    dq = jnp.zeros((length, LANES), F32)
    for h in range(heads):
        dq = jnp.where(head_lanes(lane, h), acc[h], dq)
    low = (dq * DH**-0.5).astype(BF)
    dq_ref[...] = low
    sums_ref[...] = jnp.broadcast_to(column_sum(low.astype(F32)), sums_ref.shape)
    step = width // 2
    low_o = o_ref[...].astype(BF)

    for i in range(2):
        here = slice(i * step, (i + 1) * step)
        full[here, :] = pack_pair(tn(n1_ref[:, here], low), tn(da_ref[:, here], low_o))

    pack(idx, full, outs)


def key_kernel(n_far, *refs):
    far_refs, refs = refs[:n_far], refs[n_far:]
    k_ref, v_ref, q_ref, pay_ref, dq_ref, dkv_ref, qall, pall, acc_k, acc_v = refs
    length = pay_ref.shape[0]
    heads = DELTA // DH
    pall[:length, :] = pay_ref[...]
    for j, ref in enumerate(far_refs):
        pall[(j + 1) * length : (j + 2) * length, :] = tn(ref[...], chosen()).astype(BF)
    lane = lanes_of(length)
    for j in range(n_far + 1):
        here = slice(j * length, (j + 1) * length)
        qall[here, :] = jnp.where(lane < DELTA, q_ref[here, :], pall[here, :])
    chunk = qall.shape[0] // 4
    k, v = k_ref[...], v_ref[...]
    zero, one = jnp.zeros_like(k), jnp.ones_like(k)
    for h in range(heads):
        mask = head_lanes(lane, h)
        left_k = jnp.where(mask, k, jnp.where(piece_lanes(lane, LSE, h), one, zero))
        left_v = jnp.where(mask, v, jnp.where(piece_lanes(lane, DELTA, h), one, zero))
        for j in range(4):
            here = slice(j * chunk, (j + 1) * chunk)
            p = jnp.exp(nt(left_k, qall[here, :]))
            ds = (p * nt(left_v, pall[here, :])).astype(BF)
            part_v = nn(p.astype(BF), pall[here, :])
            part_k = nn(ds, qall[here, :])
            if j == 0:
                acc_v[h] = part_v
                acc_k[h] = part_k
            else:
                acc_v[h] += part_v
                acc_k[h] += part_k
    dk = jnp.zeros((length, LANES), F32)
    dv = jnp.zeros((length, LANES), F32)
    for h in range(heads):
        dk = jnp.where(head_lanes(lane, h), acc_k[h], dk)
        dv = jnp.where(head_lanes(lane, h), acc_v[h], dv)
    dkv_ref[:, :LANES] = dq_ref[...]
    dkv_ref[:, LANES : 2 * LANES] = dk.astype(BF)
    dkv_ref[:, 2 * LANES :] = dv.astype(BF)


def back_kernel(idx, dkv_ref, w_ref, x_ref, dn0, dn1, sums_ref):
    length, width = x_ref.shape
    rows = length // 2
    sums_ref[...] = jnp.zeros_like(sums_ref)

    @pl.loop(0, 2)
    def _(i):
        here = pl.ds(pl.multiple_of(i * rows, rows), rows)
        dn = nt(dkv_ref[here, :], w_ref[:, :width])
        put_halves(idx, i, dn0, dn1, dn.astype(BF))
        xhat, _ = normalized(x_ref[here, :].astype(F32))
        sums_ref[0:1, :] += column_sum(dn * xhat)
        sums_ref[2:3, :] += column_sum(dn)


def key_grad_kernel(idx, dkv_ref, n1_ref, sums2_ref, hid_ref, dqs_ref, place_ref, *refs):
    outs, (full, little) = refs[:-2], refs[-2:]
    width = n1_ref.shape[1]
    little[...] = jnp.zeros_like(little)
    little[1:2, :] = sums2_ref[0:1, :]
    little[3:6, :] = sums2_ref[1:4, :]
    little[6:7, :] = hid_ref[...]
    col = column_sum(dkv_ref[:, 2 * LANES :].astype(F32))
    heads_row = jnp.concatenate([dqs_ref[0:1, :], col], axis=1)
    row = lax.broadcasted_iota(jnp.int32, (128, 2 * LANES), 0)
    heads_row = jnp.where(row == 7, heads_row, 0.0).astype(BF)
    full[:, 2 * DELTA :] = (jnp.transpose(little[...]) + nt(place_ref[...], heads_row)).astype(BF)
    step = width // 2
    for i in range(2):
        here = slice(i * step, (i + 1) * step)
        n1 = n1_ref[:, here]
        full[here, : 2 * DELTA] = pack_pair(tn(n1, dkv_ref[:, LANES : 2 * LANES]), tn(n1, dkv_ref[:, 2 * LANES :]))

    pack(idx, full, outs)


def add_kernel(sizes, with_norm, idx, *refs):
    groups, refs = split(refs, sizes)
    if with_norm:
        sums_ref, refs = refs[0], refs[1:]
        refs, pad, cols = refs[:-2], refs[-2], refs[-1]
        pad[...] = jnp.zeros_like(pad)
        pad[:8, :] = sums_ref[...]
        cols[...] = jnp.transpose(pad[...])
    f, c = idx[0], idx[1]
    n_c, rows = len(refs), refs[0].shape[0]
    for b in range(n_c):
        at = 0
        for group in groups:
            total = group[0][b].astype(F32)
            for ref in group[1:]:
                total = total + ref[b].astype(F32)
            wide = total.shape[1]
            if with_norm and group is groups[-1]:
                place = f * n_c + lax.rem(c + b, n_c)
                extra = cols[pl.ds(pl.multiple_of(place * rows, rows), rows), :]
                refs[b][:, at : at + wide - 128] = total[:, :-128].astype(BF)
                refs[b][:, at + wide - 128 : at + wide] = (total[:, -128:] + extra).astype(BF)
            else:
                refs[b][:, at : at + wide] = total.astype(BF)
            at += wide


def last_kernel(idx, x_ref, a_ref, b_ref, dm_ref, vec_ref, out_ref):
    rows = x_ref.shape[0] // 2
    gain = vec_ref[0:1, :]

    @pl.loop(0, 2)
    def _(i):
        here = pl.ds(pl.multiple_of(i * rows, rows), rows)
        xhat, rstd = normalized(x_ref[here, :].astype(F32))
        dn = summed(idx, i, a_ref, b_ref)
        out_ref[here, :] = (dm_ref[here, :] + norm_back(dn, gain, xhat, rstd)).astype(BF)


def out_kernel(idx, m_ref, a_ref, b_ref, vec_ref, out_ref):
    rows = m_ref.shape[0] // 2
    outb = vec_ref[5:6, :]

    @pl.loop(0, 2)
    def _(i):
        here = pl.ds(pl.multiple_of(i * rows, rows), rows)
        out_ref[here, :] = (m_ref[here, :] + summed(idx, i, a_ref, b_ref) + outb).astype(BF)


def total_kernel(local, each, *refs):
    ins, (qkv_ref, out_ref, head_ref, hid_ref, gain_ref, bias_ref, outb_ref) = refs[:-7], refs[-7:]
    total = ins[0][...].astype(F32)
    for ref in ins[1:]:
        total = total + ref[...].astype(F32)
    rows = total.shape[0]
    first, second = total[:, : 2 * local], total[:, 2 * local : 4 * local]
    qkv_ref[0] = first[:, :local]
    qkv_ref[1] = second[:, :local]
    qkv_ref[2] = pltpu.roll(second, local, 1)[:, :local]
    low = jnp.zeros((128 - rows, 2 * LANES), F32)
    mixed = jnp.concatenate([pltpu.roll(first, local, 1)[:, :LANES], total[:, 4 * local :], total[:, 4 * local :]], axis=1)
    flat = jnp.transpose(jnp.concatenate([mixed, low], axis=0))
    out_ref[...] = flat[:local, :rows]
    little = flat[LANES : LANES + 8, :rows]
    head_ref[...] = little[7:8, :each]
    hid_ref[...] = little[6:7, :]
    gain_ref[...] = little[0:2, :]
    bias_ref[...] = little[2:4, :]
    outb_ref[...] = little[4:6, :]


def body(
    frames, w_qkv, w_out, w_fc1, w_fc2, head_bias, hidden_bias, ln_gain, ln_bias, out_bias, cotangent
):
    n_f, n_c, n_t = lax.axis_size("fsdp"), lax.axis_size("ctx"), lax.axis_size("tp")
    _, length, width = frames.shape
    piece, local = w_qkv.shape[1], w_qkv.shape[2]
    blocks = n_f * n_c
    aligned = piece % 16 == 0
    f, t = lax.axis_index("fsdp"), lax.axis_index("tp")
    idx = jnp.stack([f, lax.axis_index("ctx"), t & 1, t]).astype(jnp.int32)
    x, cot = frames[0], cotangent[0]
    each = 2 * local // blocks
    place = np.zeros((width, 2 * LANES), np.float32)
    for b in range(blocks):
        for r in range(each):
            at = b * each + r
            place[b * piece + r, at % local + at // local * LANES] = 1
    place = jnp.asarray(place, BF)

    together = length // n_t == piece
    outs = (shape(piece, width + 128),) + (shape(piece, 2 * width + 128),) * together
    small = (ln_gain, ln_bias, out_bias, hidden_bias, head_bias)
    stay = (w_qkv, w_out, *small)
    first, *packet = call(
        first_kernel, outs, *stay, x,
        scratch=[pltpu.VMEM(a.shape, BF) for a in stay]
        + [pltpu.VMEM((length // n_t, width), BF), pltpu.SemaphoreType.DMA((len(stay) + 1,))],
        idx=idx, flops=10**9, where=pl.ANY, limit=60 * 1024 * 1024,
    )

    def near_blocks(shard):
        return [shard] + [send(shard, "ctx", k) for k in range(1, n_c)]

    def ordered(groups):
        if aligned:
            return groups
        groups = [jnp.concatenate([b if b.ndim == 3 else b[None] for b in g]) for g in groups]
        groups = jnp.stack(groups)
        return [[canonical(groups).reshape(1, width, -1)]]

    fc2_t = w_fc2.T
    own_far = [send(first, "fsdp", a) for a in range(1, n_f)]
    own1 = [send(after(w_fc1, first), "fsdp", a) for a in range(1, n_f)]
    if together:
        near = near_blocks(packet[0])[1:]
        near, far = [b[:, : first.shape[1]] for b in near], [b[:, first.shape[1] :] for b in near]
    else:
        quarter = lax.dynamic_slice_in_dim(x, t * (length // n_t), length // n_t, 0)
        near, far = near_blocks(first)[1:], near_blocks(quarter)[1:]
    near, far, own_far, own1 = lax.optimization_barrier((near, far, own_far, own1))
    far, rest = jnp.stack(far), jnp.stack(near)
    near = [first] + near
    rest_far = [send(rest, "fsdp", a) for a in range(1, n_f)]
    w_groups = ordered([near] + [[a, b] for a, b in zip(own_far, rest_far)])
    quarters = {0: far}
    bit = n_t // 2
    while bit > 0:
        for mask in list(quarters):
            quarters[mask ^ bit] = flip(quarters[mask], "tp", bit)
        bit //= 2
    quarters = {mask: [q] for mask, q in quarters.items()}
    masks = tuple(quarters)
    def sizes(groups):
        return tuple(len(g) for g in groups)

    def flat(groups):
        return [r for g in groups for r in g]

    halves = (shape(length // 2, width), shape(length // 2, width))
    rows_of = shape(length, LANES)
    w_all, wo, vec, n1, q_own, k_own, v_own = call(
        functools.partial(own_kernel, sizes(w_groups)),
        (
            shape(width, width + 128), shape(width, LANES), shape(8, width, dtype=F32),
            shape(length, width), rows_of, rows_of, rows_of,
        ),
        *flat(w_groups), x, place,
        idx=idx, flops=6 * 10**9,
    )
    near1 = [w_fc1] + near_blocks(after(w_fc1, far))[1:]
    rest1 = jnp.stack(after(near1[1:], vec))
    fc1 = ordered([near1] + [[a, send(rest1, "fsdp", k + 1)] for k, a in enumerate(own1)])
    own2 = [send(after(fc2_t, rest_far), "fsdp", a) for a in range(1, n_f)]
    near2 = [fc2_t] + near_blocks(after(fc2_t, rest1, quarters))[1:]
    rest2 = jnp.stack(near2[1:])
    fc2 = ordered([near2] + [[a, send(rest2, "fsdp", k + 1)] for k, a in enumerate(own2)])

    total = n_c * length
    every = shape(total, LANES)
    q_groups = list(quarters.values())
    q, k, v, o, aux, *branch = call(
        functools.partial(attend_kernel, masks, sizes(q_groups)),
        (every, every, every, shape(length, LANES, dtype=F32), rows_of, *halves),
        *flat(q_groups), w_all, wo, vec, place, after(q_own, rest1), k_own, v_own,
        scratch=[
            pltpu.VMEM((length, width), BF), pltpu.VMEM((length, width), BF),
            pltpu.VMEM((length, total), F32), pltpu.VMEM((length, LANES), F32),
        ],
        idx=idx, flops=14 * 10**9,
    )
    a0, a1 = tp_rest(tp_half((branch[0], after(branch[1], rest2, fc1, own2))))
    m, n2, g, df, mlp0, mlp1, dn0, dn1 = call(
        functools.partial(feed_kernel, sizes(fc1) + sizes(fc2)),
        (
            shape(length, width, dtype=F32), shape(length, width), shape(length, width),
            shape(length, width), *halves, *halves,
        ),
        *flat(fc1), *flat(fc2), x, a0, a1, cot, vec,
        scratch=[pltpu.VMEM((width, width), BF), pltpu.VMEM((width, width), BF)],
        idx=idx, flops=10 * 10**9,
    )
    dn_half = tp_half((dn0, dn1))

    def packed(cols):
        if aligned:
            return tuple(shape(n_c, piece, cols) for _ in range(n_f))
        return (shape(1, width, cols),)

    def as_blocks(parts):
        if aligned:
            return parts
        parts = relative(parts[0].reshape(n_f, n_c, piece, -1))
        return [parts[a] for a in range(n_f)]

    *gfc, hid = call(
        feed_grad_kernel,
        (*packed(width), *packed(width), shape(1, width, dtype=F32)),
        n2, after(df, dn_half), cot, g,
        scratch=[pltpu.VMEM((width, width), BF), pltpu.VMEM((width, width), BF)],
        idx=idx, flops=5 * 10**9,
    )
    b0, b1 = tp_rest(dn_half, hid)
    dm, da, pay, sent, sums2 = call(
        middle_kernel,
        (
            shape(length, width, dtype=F32), shape(length, width), shape(length, LANES),
            shape(SENT, length), shape(8, width, dtype=F32),
        ),
        m, b0, b1, cot, o, aux, wo, vec,
        idx=idx, flops=5 * 10**9,
    )
    far_pay = [send(sent, "ctx", j) for j in range(1, n_c)]

    def over_fsdp(parts):
        parts = as_blocks(parts)
        return [parts[0]] + [send(parts[a], "fsdp", a) for a in range(1, n_f)]

    def added(groups, wait, norm=None):
        groups = [[g[0], *after(g[1:], wait)] for g in groups]
        cols = sum(g[0].shape[-1] for g in groups)
        if not aligned:
            total = jnp.concatenate([sum(p.astype(F32) for p in g) for g in groups], axis=-1)
            if norm is not None:
                rows = relative(norm.T.reshape(n_f, n_c, piece, 8))[0]
                total = total.at[..., cols - 128 : cols - 120].add(rows)
            return list(total.astype(BF))
        extra = () if norm is None else (norm,)
        scratch = () if norm is None else (pltpu.VMEM((128, width), F32), pltpu.VMEM((width, 128), F32))
        return call(
            functools.partial(add_kernel, sizes(groups), norm is not None),
            tuple(shape(piece, cols) for _ in range(n_c)),
            *flat(groups), *extra,
            scratch=scratch, idx=idx, flops=10**9,
        )

    def over_ctx(low):
        return [low[0]] + [send(low[j], "ctx", j) for j in range(1, n_c)]

    def sum_of(parts):
        return sum(p.astype(F32) for p in parts)

    gfc1 = over_fsdp(gfc[: len(gfc) // 2])
    gfc2 = over_fsdp([after(p, gfc1) for p in gfc[len(gfc) // 2 :]])
    *gr_q, dq, dq_sum = call(
        query_kernel,
        (*packed(2 * local), rows_of, shape(8, LANES, dtype=F32)),
        q_own, pay, k, v, n1, da, o,
        scratch=[pltpu.VMEM((width, 2 * local), BF), pltpu.VMEM((DELTA // DH, length, LANES), F32)],
        idx=idx, flops=0,
    )
    gfc1 = over_ctx(after(added([gfc1], dq), far_pay))
    y0, y1 = tp_rest(tp_half((mlp0, after(mlp1, pay))))
    (dkv,) = call(
        functools.partial(key_kernel, n_c - 1),
        (shape(length, 3 * LANES),),
        *far_pay, k_own, v_own, q, after(pay, gfc1[0], y0), dq,
        scratch=[
            pltpu.VMEM((total, LANES), BF), pltpu.VMEM((total, LANES), BF),
            pltpu.VMEM((DELTA // DH, length, LANES), F32), pltpu.VMEM((DELTA // DH, length, LANES), F32),
        ],
        flops=12 * 10**9,
    )
    gr_q = over_fsdp([after(p, gfc2) for p in gr_q])
    grads = call(
        key_grad_kernel,
        packed(2 * local + 128),
        dkv, n1, sums2, hid, dq_sum, place,
        scratch=[pltpu.VMEM((width, 2 * local + 128), BF), pltpu.VMEM((128, width), F32)],
        idx=idx, flops=2 * 10**9,
    )
    dx0, dx1, sums1 = call(
        back_kernel, (*halves, shape(8, width, dtype=F32)), after(dkv, grads, gfc1, gfc2), w_all, x,
        idx=idx, flops=2 * 10**9,
    )
    grads = over_fsdp(grads)
    sums1 = sums_over(sums1, "tp")
    gfc2_low = added([gfc2], dx1)
    gfc2 = over_ctx(gfc2_low)
    sums1 = sums_over(after(sums1, gfc2_low, grads, gr_q), "fsdp")
    e_half = tp_half((dx0, dx1))
    rest = over_ctx(added([gr_q, grads], (gfc2), sums1))
    output = call(
        out_kernel, (shape(length, width),), m, y0, y1, vec, idx=idx, flops=2 * 10**9
    )[0]
    e0, e1 = tp_rest(e_half)
    input_grad = call(
        last_kernel, (shape(length, width),), x, e0, e1, dm, vec, idx=idx, flops=3 * 10**9
    )[0]

    fc1_grad, fc2_grad = sum_of(gfc1), sum_of(gfc2).T
    if aligned:
        qkv_grad, out_grad, head, hidden, gain, bias, outb = call(
            functools.partial(total_kernel, local, each),
            tuple(
                shape(*dims, dtype=F32)
                for dims in (
                    (3, piece, local), (local, piece), (1, each), (1, piece), (2, piece), (2, piece), (2, piece),
                )
            ),
            *rest,
            flops=2 * 10**9,
        )
    else:
        sums = sum_of(rest)
        cuts = [sums[:, j * local : (j + 1) * local] for j in range(4)]
        little = sums[:, 4 * local : 4 * local + 8].T
        qkv_grad, out_grad = jnp.stack([cuts[0], cuts[2], cuts[3]]), cuts[1].T
        head, hidden = little[7:8, :each], little[6:7]
        gain, bias, outb = little[0:2], little[2:4], little[4:6]
    return (
        output[None], input_grad[None], qkv_grad, out_grad, fc1_grad, fc2_grad, head, hidden, gain, bias, outb,
    )


def solution(mesh):
    shards = ("fsdp", "ctx")
    rows = P("fsdp", "ctx", None)
    qkv = P(None, shards, "tp")
    by_tp = P("tp", shards)
    norm = P(None, shards)
    weights = (qkv, by_tp, P(shards, "tp"), by_tp, by_tp, by_tp, norm, norm, norm)
    return jax.shard_map(
        body,
        mesh=mesh,
        in_specs=(rows, *weights, rows),
        out_specs=(rows, rows, *weights),
        check_vma=False,
    )
```

```python
import functools

import jax
import jax.numpy as jnp
import numpy as np
from jax import lax
from jax.experimental import pallas as pl
from jax.experimental.pallas import tpu as pltpu
from jax.sharding import PartitionSpec as P

DH = 64
EPS = 1e-05
BF = jnp.bfloat16
F32 = jnp.float32
LANES = 256
DELTA = 192
LSE = 198
SENT = 208
VMEM_LIMIT = 20 * 1024 * 1024


def ring(axis, k):
    n = lax.axis_size(axis)
    return [(i, (i + k) % n) for i in range(n)]


def send(x, axis, k):
    return lax.ppermute(x, axis, ring(axis, k))


def flip(x, axis, bit):
    return lax.ppermute(x, axis, [(i, i ^ bit) for i in range(lax.axis_size(axis))])


def after(x, *others):
    return lax.optimization_barrier((x, others))[0]


def add_low(a, b):
    return (a.astype(F32) + b.astype(F32)).astype(BF)


def tp_half(both):
    return add_low(both[0], flip(both[1], "tp", 1))


def tp_rest(half, wait=()):
    bit = 2
    while bit < lax.axis_size("tp"):
        half = add_low(half, after(flip(half, "tp", bit), wait))
        bit *= 2
    return half, flip(half, "tp", 1)


def sums_over(x, axis):
    bit = 1
    while bit < lax.axis_size(axis):
        x = x + flip(x, axis, bit)
        bit *= 2
    return x


def turned(x, shift, axis):
    n = x.shape[axis]
    return jnp.take(x, (shift - jnp.arange(n)) % n, axis=axis)


def canonical(blocks):
    return turned(turned(blocks, lax.axis_index("fsdp"), 0), lax.axis_index("ctx"), 1)


def relative(blocks):
    f, c = lax.axis_index("fsdp"), lax.axis_index("ctx")
    blocks = jnp.take(blocks, (f + jnp.arange(blocks.shape[0])) % blocks.shape[0], axis=0)
    return jnp.take(blocks, (c + jnp.arange(blocks.shape[1])) % blocks.shape[1], axis=1)


def dot(a, b, da, db):
    return lax.dot_general(a, b, (((da,), (db,)), ((), ())), preferred_element_type=F32)


def nn(a, b):
    return dot(a, b, 1, 0)


def nt(a, b):
    return dot(a, b, 1, 1)


def tn(a, b):
    return dot(a, b, 0, 0)


def lanes_of(rows):
    return lax.broadcasted_iota(jnp.int32, (rows, LANES), 1)


def head_lanes(lane, h):
    return (lane >= h * DH) & (lane < (h + 1) * DH)


def piece_lanes(lane, first, h):
    count = 2 if first == DELTA else 3
    return (lane >= first + count * h) & (lane < first + count * (h + 1))


def in_pieces(lane, first, h, column):
    count = 2 if first == DELTA else 3
    out = jnp.zeros(lane.shape, F32)
    rest = column
    for j in range(count):
        piece = rest.astype(BF).astype(F32)
        out = jnp.where(lane == first + count * h + j, piece, out)
        rest = rest - piece
    return out


def chosen():
    row = lax.broadcasted_iota(jnp.int32, (SENT, LANES), 0)
    lane = lax.broadcasted_iota(jnp.int32, (SENT, LANES), 1)
    return jnp.where(row == lane, 1.0, 0.0).astype(BF)


def normalized(x):
    mean = jnp.mean(x, axis=-1, keepdims=True)
    centered = x - mean
    var = jnp.mean(centered * centered, axis=-1, keepdims=True)
    rstd = lax.rsqrt(var + EPS)
    return centered * rstd, rstd


def norm_back(grad, gain, xhat, rstd):
    dx = grad * gain
    return rstd * (
        dx
        - jnp.mean(dx, axis=-1, keepdims=True)
        - xhat * jnp.mean(dx * xhat, axis=-1, keepdims=True)
    )


def column_sum(x):
    return jnp.sum(x, axis=0, keepdims=True)


def call(kernel, outs, *args, scratch=(), flops=0, idx=None, where=pltpu.VMEM, limit=VMEM_LIMIT):
    ins = [pl.BlockSpec(memory_space=where) for _ in args]
    if idx is not None:
        ins = [pl.BlockSpec(memory_space=pltpu.SMEM)] + ins
        args = (idx, *args)
    moved = sum(a.size * a.dtype.itemsize for a in args)
    moved += sum(o.size * o.dtype.itemsize for o in outs)
    return pl.pallas_call(
        kernel,
        out_shape=tuple(outs),
        in_specs=ins,
        out_specs=tuple(pl.BlockSpec(memory_space=pltpu.VMEM) for _ in outs),
        scratch_shapes=list(scratch),
        compiler_params=pltpu.CompilerParams(vmem_limit_bytes=limit),
        cost_estimate=pl.CostEstimate(flops=flops, bytes_accessed=moved, transcendentals=0),
    )(*args)


def shape(*dims, dtype=BF):
    return jax.ShapeDtypeStruct(dims, dtype)


def listed(groups):
    out = []
    for refs in groups:
        blocks = []
        for ref in refs:
            blocks += [ref.at[j] for j in range(ref.shape[0])] if len(ref.shape) == 3 else [ref]
        out.append(blocks)
    return out


def unpack(idx, groups, out_ref):
    f, c = idx[0], idx[1]
    groups = listed(groups)
    n_f, n_c, rows = len(groups), len(groups[0]), groups[0][0].shape[0]
    for a in range(n_f):
        for b in range(n_c):
            at = lax.rem(f - a + n_f, n_f) * n_c + lax.rem(c - b + n_c, n_c)
            out_ref[pl.ds(pl.multiple_of(at * rows, rows), rows), :] = groups[a][b][...]


def pack(idx, full_ref, refs):
    f, c = idx[0], idx[1]
    n_f, (n_c, rows, _) = len(refs), refs[0].shape
    for a in range(n_f):
        for b in range(n_c):
            at = lax.rem(f + a, n_f) * n_c + lax.rem(c + b, n_c)
            refs[a][b] = full_ref[pl.ds(pl.multiple_of(at * rows, rows), rows), :]


def split(refs, sizes):
    out = []
    for size in sizes:
        out.append(refs[:size])
        refs = refs[size:]
    return out, refs


def project(n1_ref, w_ref, hb, q_ref, k_ref, v_ref, at):
    rows, width = n1_ref.shape
    lane = lanes_of(rows)
    here = slice(at, at + rows)
    n1 = n1_ref[...]
    q = ((nn(n1, w_ref[:, :LANES]) + hb[:, :LANES]).astype(BF)) * jnp.asarray(DH**-0.5, BF)
    q_ref[here, :] = jnp.where(lane < DELTA, q, jnp.zeros_like(q))
    k = nn(n1, w_ref[:, LANES : 2 * LANES]).astype(BF)
    k_ref[here, :] = jnp.where(lane < DELTA, k, jnp.ones_like(k))
    v = (nn(n1, w_ref[:, 2 * LANES : width]) + hb[:, LANES:]).astype(BF)
    v_ref[here, :] = jnp.where(lane < DELTA, v, jnp.ones_like(v))


def norm_rows(x_ref, gain, shift, out_ref, rows):
    @pl.loop(0, x_ref.shape[0] // rows)
    def _(i):
        here = pl.ds(pl.multiple_of(i * rows, rows), rows)
        xhat, _ = normalized(x_ref[here, :].astype(F32))
        out_ref[here, :] = (xhat * gain + shift).astype(BF)


def first_kernel(
    idx, w_any, out_any, gain_any, bias_any, outb_any, hid_any, head_any, x_any, first_ref, *refs
):
    packet_ref, (w_ref, out_ref, *vectors, x_ref, sems) = refs[:-9], refs[-9:]
    rows = x_ref.shape[0]
    pairs = [
        (w_any, w_ref), (out_any, out_ref), *zip((gain_any, bias_any, outb_any, hid_any, head_any), vectors),
        (x_any.at[pl.ds(pl.multiple_of(idx[3] * rows, rows), rows), :], x_ref),
    ]
    copies = [pltpu.make_async_copy(a, b, sems.at[k]) for k, (a, b) in enumerate(pairs)]
    for copy in copies:
        copy.start()
    for copy in copies:
        copy.wait()
    local = w_ref.shape[2]
    third = local // 3
    at = lax.broadcasted_iota(jnp.int32, (local, LANES), 0)
    lane = lax.broadcasted_iota(jnp.int32, (local, LANES), 1)
    keep = jnp.where(at == lane, 1.0, 0.0).astype(BF)
    for j in range(3):
        move = jnp.where((lane >= local) & (at == lane - local + j * third), 1.0, 0.0).astype(BF)
        first_ref[:, j * LANES : (j + 1) * LANES] = (nn(w_ref[j], keep) + tn(out_ref[...], move)).astype(BF)
    columns = jnp.zeros((first_ref.shape[0], 128), F32)
    begin = 0
    for ref in vectors:
        count, size = ref.shape
        vec = ref[...]
        if size < first_ref.shape[0]:
            row = lax.broadcasted_iota(jnp.int32, (size, first_ref.shape[0]), 0)
            col = lax.broadcasted_iota(jnp.int32, (size, first_ref.shape[0]), 1)
            vec = nn(vec, jnp.where(row == col, 1.0, 0.0).astype(BF)).astype(BF)
        at = lax.broadcasted_iota(jnp.int32, (count, 128), 0)
        lane = lax.broadcasted_iota(jnp.int32, (count, 128), 1)
        columns = columns + tn(vec, jnp.where(lane == at + begin, 1.0, 0.0).astype(BF))
        begin += count
    first_ref[:, 3 * LANES :] = columns.astype(BF)
    for ref in packet_ref:
        ref[:, : first_ref.shape[1]] = first_ref[...]
        ref[:, first_ref.shape[1] :] = x_ref[...]


def own_kernel(sizes, idx, *refs):
    groups, refs = split(refs, sizes)
    x_ref, place_ref, w_ref, wo_ref, vec_ref, n1_ref, q_ref, k_ref, v_ref = refs
    unpack(idx, groups, w_ref)
    length, width = x_ref.shape
    heads = DELTA // DH
    step = 128
    lane = lanes_of(step)
    vec = jnp.transpose(w_ref[:, width:].astype(F32))[:8, :]
    vec_ref[...] = vec
    hb = nn(vec.astype(BF), place_ref[...])[7:8, :]
    norm_rows(x_ref, vec[0:1, :], vec[2:3, :], n1_ref, length // 4)
    project(n1_ref, w_ref, hb, q_ref, k_ref, v_ref, 0)

    @pl.loop(0, width // step)
    def _(i):
        here = pl.ds(pl.multiple_of(i * step, step), step)
        out = jnp.zeros((step, LANES), F32)
        for h in range(heads):
            group = w_ref[here, h * LANES : (h + 1) * LANES].astype(F32)
            out = jnp.where(head_lanes(lane, h), pltpu.roll(group, (h + 1) * DH, 1), out)
        wo_ref[here, :] = out.astype(BF)


def attend_kernel(masks, sizes, idx, *refs):
    groups, refs = split(refs, sizes)
    groups = listed(groups)
    w_ref, wo_ref, vec_ref, place_ref, qo_ref, ko_ref, vo_ref = refs[:7]
    q_ref, k_ref, v_ref, o_ref, aux_ref, mine_ref, other_ref, x_scr, n_scr, s_scr, acc = refs[7:]
    length = qo_ref.shape[0]
    total = k_ref.shape[0]
    heads = DELTA // DH
    vec = vec_ref[...]
    hb = nn(vec.astype(BF), place_ref[...])[7:8, :]
    q_ref[:length, :] = qo_ref[...]
    k_ref[:length, :] = ko_ref[...]
    v_ref[:length, :] = vo_ref[...]
    piece = groups[0][0].shape[0]
    for j in range(len(groups[0])):
        for mask, group in zip(masks, groups):
            at = lax.bitwise_xor(idx[3], mask) * piece
            x_scr[pl.ds(pl.multiple_of(at, piece), piece), :] = group[j][...]
        norm_rows(x_scr, vec[0:1, :], vec[2:3, :], n_scr, length // 4)
        project(n_scr, w_ref, hb, q_ref, k_ref, v_ref, (j + 1) * length)

    lane = lanes_of(length)
    chunk = total // 4
    o_ref[...] = jnp.zeros_like(o_ref)
    aux_ref[...] = jnp.zeros_like(aux_ref)
    for h in range(heads):
        mask = head_lanes(lane, h)
        q = jnp.where(mask, qo_ref[...], jnp.zeros((length, LANES), BF))
        top = jnp.full((length, 128), -jnp.inf, F32)
        for j in range(4):
            here = slice(j * chunk, (j + 1) * chunk)
            s = nt(q, k_ref[here, :])
            s_scr[:, here] = s
            for i in range(chunk // 128):
                top = jnp.maximum(top, s[:, i * 128 : (i + 1) * 128])
        top = jnp.max(top, axis=-1, keepdims=True)
        for j in range(4):
            here = slice(j * chunk, (j + 1) * chunk)
            part = nn(jnp.exp(s_scr[:, here] - top).astype(BF), v_ref[here, :])
            if j == 0:
                acc[...] = part
            else:
                acc[...] += part
        ev = acc[...]
        mass = ev[:, DELTA : DELTA + 1]
        o_ref[...] = jnp.where(mask, ev / mass, o_ref[...])
        aux_ref[...] += in_pieces(lane, LSE, h, -(top + jnp.log(mass))).astype(BF)
    rows = length // 2
    put_halves(idx, 0, mine_ref, other_ref, nt(o_ref[:rows, :].astype(BF), wo_ref[...]).astype(BF))
    put_halves(idx, 1, mine_ref, other_ref, nt(o_ref[rows:, :].astype(BF), wo_ref[...]).astype(BF))


def summed(idx, i, mine_ref, other_ref):
    return jnp.where(i == idx[2], mine_ref[...].astype(F32), other_ref[...].astype(F32))


def put_halves(idx, i, mine_ref, other_ref, value):
    @pl.when(i == idx[2])
    def _():
        mine_ref[...] = value

    @pl.when(i != idx[2])
    def _():
        other_ref[...] = value


def feed_kernel(sizes, idx, *refs):
    groups, refs = split(refs, sizes)
    x_ref, a_ref, b_ref, c_ref, vec_ref = refs[:5]
    m_ref, n2_ref, g_ref, df_ref, mlp0, mlp1, dn0, dn1, w1_ref, w2_ref = refs[5:]
    unpack(idx, groups[: len(groups) // 2], w1_ref)
    unpack(idx, groups[len(groups) // 2 :], w2_ref)
    rows = x_ref.shape[0] // 2
    gain, shift, outb, hidb = vec_ref[1:2, :], vec_ref[3:4, :], vec_ref[4:5, :], vec_ref[6:7, :]

    @pl.loop(0, 2)
    def _(i):
        here = pl.ds(pl.multiple_of(i * rows, rows), rows)
        m = x_ref[here, :].astype(F32) + (summed(idx, i, a_ref, b_ref) + outb)
        m_ref[here, :] = m
        xhat, _ = normalized(m)
        n2 = (xhat * gain + shift).astype(BF)
        n2_ref[here, :] = n2
        f = nn(n2, w1_ref[...]) + hidb
        cdf = 0.5 * (1.0 + lax.erf(f * (0.5**0.5)))
        g = (f * cdf).astype(BF)
        g_ref[here, :] = g
        dg = nn(c_ref[here, :], w2_ref[...])
        slope = cdf + f * (jnp.exp(-0.5 * f * f) * 0.3989422804014327)
        df = (dg * slope).astype(BF)
        df_ref[here, :] = df
        put_halves(idx, i, dn0, dn1, nt(df, w1_ref[...]).astype(BF))
        put_halves(idx, i, mlp0, mlp1, nt(g, w2_ref[...]).astype(BF))


def feed_grad_kernel(idx, n2_ref, df_ref, c_ref, g_ref, *refs):
    outs, (hid_ref, full1, full2) = refs[:-3], refs[-3:]
    hid_ref[...] = column_sum(df_ref[...].astype(F32))
    step = n2_ref.shape[1] // 2

    @pl.loop(0, 2)
    def _(i):
        here = pl.ds(pl.multiple_of(i * step, step), step)
        full1[here, :] = tn(n2_ref[:, here], df_ref[...]).astype(BF)
        full2[here, :] = tn(c_ref[:, here], g_ref[...]).astype(BF)

    pack(idx, full1, outs[: len(outs) // 2])
    pack(idx, full2, outs[len(outs) // 2 :])


def middle_kernel(
    idx, m_ref, a_ref, b_ref, c_ref, o_ref, aux_ref, wo_ref, vec_ref,
    dm_ref, da_ref, pay_ref, sent_ref, sums_ref,
):
    rows = m_ref.shape[0] // 2
    heads = DELTA // DH
    gain = vec_ref[1:2, :]
    lane = lanes_of(rows)
    sums_ref[...] = jnp.zeros_like(sums_ref)

    @pl.loop(0, 2)
    def _(i):
        here = pl.ds(pl.multiple_of(i * rows, rows), rows)
        xhat, rstd = normalized(m_ref[here, :])
        dn = summed(idx, i, a_ref, b_ref)
        c = c_ref[here, :].astype(F32)
        dm = c + norm_back(dn, gain, xhat, rstd)
        dm_ref[here, :] = dm
        da = dm.astype(BF)
        da_ref[here, :] = da
        do = nn(da, wo_ref[...]).astype(BF)
        prod = do.astype(F32) * o_ref[here, :]
        extra = aux_ref[here, :].astype(F32)
        for h in range(heads):
            delta = jnp.sum(jnp.where(head_lanes(lane, h), prod, 0.0), axis=-1, keepdims=True)
            extra = extra + in_pieces(lane, DELTA, h, -delta)
        pay_ref[here, :] = jnp.where(lane < DELTA, do, extra.astype(BF))
        sums_ref[0:1, :] += column_sum(dn * xhat)
        sums_ref[1:2, :] += column_sum(dn)
        sums_ref[2:3, :] += column_sum(da.astype(F32))
        sums_ref[3:4, :] += column_sum(c)

    sent_ref[...] = nt(chosen(), pay_ref[...]).astype(BF)


def pack_pair(first, second):
    lane = lanes_of(first.shape[0])
    moved = pltpu.roll(second, DELTA, 1)
    return jnp.concatenate([jnp.where(lane < DELTA, first, moved), moved[:, :128]], axis=1).astype(BF)


def query_kernel(idx, q_ref, pay_ref, k_ref, v_ref, n1_ref, da_ref, o_ref, *refs):
    outs, (dq_ref, sums_ref, full, acc) = refs[:-4], refs[-4:]
    length, width = n1_ref.shape
    total = k_ref.shape[0]
    heads = DELTA // DH
    lane = lanes_of(length)
    chunk = total // 4
    pay = pay_ref[...]
    q = jnp.where(lane < DELTA, q_ref[...], pay)
    zero = jnp.zeros_like(q)
    for h in range(heads):
        mask = head_lanes(lane, h)
        left_q = jnp.where(mask | piece_lanes(lane, LSE, h), q, zero)
        left_p = jnp.where(mask | piece_lanes(lane, DELTA, h), pay, zero)
        for j in range(4):
            here = slice(j * chunk, (j + 1) * chunk)
            p = jnp.exp(nt(left_q, k_ref[here, :]))
            ds = (p * nt(left_p, v_ref[here, :])).astype(BF)
            part = nn(ds, k_ref[here, :])
            if j == 0:
                acc[h] = part
            else:
                acc[h] += part
    dq = jnp.zeros((length, LANES), F32)
    for h in range(heads):
        dq = jnp.where(head_lanes(lane, h), acc[h], dq)
    low = (dq * DH**-0.5).astype(BF)
    dq_ref[...] = low
    sums_ref[...] = jnp.broadcast_to(column_sum(low.astype(F32)), sums_ref.shape)
    step = width // 2
    low_o = o_ref[...].astype(BF)

    for i in range(2):
        here = slice(i * step, (i + 1) * step)
        full[here, :] = pack_pair(tn(n1_ref[:, here], low), tn(da_ref[:, here], low_o))

    pack(idx, full, outs)


def key_kernel(n_far, *refs):
    far_refs, refs = refs[:n_far], refs[n_far:]
    k_ref, v_ref, q_ref, pay_ref, dq_ref, dkv_ref, qall, pall, acc_k, acc_v = refs
    length = pay_ref.shape[0]
    heads = DELTA // DH
    pall[:length, :] = pay_ref[...]
    for j, ref in enumerate(far_refs):
        pall[(j + 1) * length : (j + 2) * length, :] = tn(ref[...], chosen()).astype(BF)
    lane = lanes_of(length)
    for j in range(n_far + 1):
        here = slice(j * length, (j + 1) * length)
        qall[here, :] = jnp.where(lane < DELTA, q_ref[here, :], pall[here, :])
    chunk = qall.shape[0] // 4
    k, v = k_ref[...], v_ref[...]
    zero, one = jnp.zeros_like(k), jnp.ones_like(k)
    for h in range(heads):
        mask = head_lanes(lane, h)
        left_k = jnp.where(mask, k, jnp.where(piece_lanes(lane, LSE, h), one, zero))
        left_v = jnp.where(mask, v, jnp.where(piece_lanes(lane, DELTA, h), one, zero))
        for j in range(4):
            here = slice(j * chunk, (j + 1) * chunk)
            p = jnp.exp(nt(left_k, qall[here, :]))
            ds = (p * nt(left_v, pall[here, :])).astype(BF)
            part_v = nn(p.astype(BF), pall[here, :])
            part_k = nn(ds, qall[here, :])
            if j == 0:
                acc_v[h] = part_v
                acc_k[h] = part_k
            else:
                acc_v[h] += part_v
                acc_k[h] += part_k
    dk = jnp.zeros((length, LANES), F32)
    dv = jnp.zeros((length, LANES), F32)
    for h in range(heads):
        dk = jnp.where(head_lanes(lane, h), acc_k[h], dk)
        dv = jnp.where(head_lanes(lane, h), acc_v[h], dv)
    dkv_ref[:, :LANES] = dq_ref[...]
    dkv_ref[:, LANES : 2 * LANES] = dk.astype(BF)
    dkv_ref[:, 2 * LANES :] = dv.astype(BF)


def back_kernel(idx, dkv_ref, w_ref, x_ref, dn0, dn1, sums_ref):
    length, width = x_ref.shape
    rows = length // 2
    sums_ref[...] = jnp.zeros_like(sums_ref)

    @pl.loop(0, 2)
    def _(i):
        here = pl.ds(pl.multiple_of(i * rows, rows), rows)
        dn = nt(dkv_ref[here, :], w_ref[:, :width])
        put_halves(idx, i, dn0, dn1, dn.astype(BF))
        xhat, _ = normalized(x_ref[here, :].astype(F32))
        sums_ref[0:1, :] += column_sum(dn * xhat)
        sums_ref[2:3, :] += column_sum(dn)


def key_grad_kernel(idx, dkv_ref, n1_ref, sums2_ref, hid_ref, dqs_ref, place_ref, *refs):
    outs, (full, little) = refs[:-2], refs[-2:]
    width = n1_ref.shape[1]
    little[...] = jnp.zeros_like(little)
    little[1:2, :] = sums2_ref[0:1, :]
    little[3:6, :] = sums2_ref[1:4, :]
    little[6:7, :] = hid_ref[...]
    col = column_sum(dkv_ref[:, 2 * LANES :].astype(F32))
    heads_row = jnp.concatenate([dqs_ref[0:1, :], col], axis=1)
    row = lax.broadcasted_iota(jnp.int32, (128, 2 * LANES), 0)
    heads_row = jnp.where(row == 7, heads_row, 0.0).astype(BF)
    full[:, 2 * DELTA :] = (jnp.transpose(little[...]) + nt(place_ref[...], heads_row)).astype(BF)
    step = width // 2
    for i in range(2):
        here = slice(i * step, (i + 1) * step)
        n1 = n1_ref[:, here]
        full[here, : 2 * DELTA] = pack_pair(tn(n1, dkv_ref[:, LANES : 2 * LANES]), tn(n1, dkv_ref[:, 2 * LANES :]))

    pack(idx, full, outs)


def add_kernel(sizes, with_norm, idx, *refs):
    groups, refs = split(refs, sizes)
    if with_norm:
        sums_ref, refs = refs[0], refs[1:]
        refs, pad, cols = refs[:-2], refs[-2], refs[-1]
        pad[...] = jnp.zeros_like(pad)
        pad[:8, :] = sums_ref[...]
        cols[...] = jnp.transpose(pad[...])
    f, c = idx[0], idx[1]
    n_c, rows = len(refs), refs[0].shape[0]
    for b in range(n_c):
        at = 0
        for group in groups:
            total = group[0][b].astype(F32)
            for ref in group[1:]:
                total = total + ref[b].astype(F32)
            wide = total.shape[1]
            if with_norm and group is groups[-1]:
                place = f * n_c + lax.rem(c + b, n_c)
                extra = cols[pl.ds(pl.multiple_of(place * rows, rows), rows), :]
                refs[b][:, at : at + wide - 128] = total[:, :-128].astype(BF)
                refs[b][:, at + wide - 128 : at + wide] = (total[:, -128:] + extra).astype(BF)
            else:
                refs[b][:, at : at + wide] = total.astype(BF)
            at += wide


def last_kernel(idx, x_ref, a_ref, b_ref, dm_ref, vec_ref, out_ref):
    rows = x_ref.shape[0] // 2
    gain = vec_ref[0:1, :]

    @pl.loop(0, 2)
    def _(i):
        here = pl.ds(pl.multiple_of(i * rows, rows), rows)
        xhat, rstd = normalized(x_ref[here, :].astype(F32))
        dn = summed(idx, i, a_ref, b_ref)
        out_ref[here, :] = (dm_ref[here, :] + norm_back(dn, gain, xhat, rstd)).astype(BF)


def out_kernel(idx, m_ref, a_ref, b_ref, vec_ref, out_ref):
    rows = m_ref.shape[0] // 2
    outb = vec_ref[5:6, :]

    @pl.loop(0, 2)
    def _(i):
        here = pl.ds(pl.multiple_of(i * rows, rows), rows)
        out_ref[here, :] = (m_ref[here, :] + summed(idx, i, a_ref, b_ref) + outb).astype(BF)


def total_kernel(local, each, *refs):
    ins, (qkv_ref, out_ref, head_ref, hid_ref, gain_ref, bias_ref, outb_ref) = refs[:-7], refs[-7:]
    total = ins[0][...].astype(F32)
    for ref in ins[1:]:
        total = total + ref[...].astype(F32)
    rows = total.shape[0]
    first, second = total[:, : 2 * local], total[:, 2 * local : 4 * local]
    qkv_ref[0] = first[:, :local]
    qkv_ref[1] = second[:, :local]
    qkv_ref[2] = pltpu.roll(second, local, 1)[:, :local]
    low = jnp.zeros((128 - rows, 2 * LANES), F32)
    mixed = jnp.concatenate([pltpu.roll(first, local, 1)[:, :LANES], total[:, 4 * local :], total[:, 4 * local :]], axis=1)
    flat = jnp.transpose(jnp.concatenate([mixed, low], axis=0))
    out_ref[...] = flat[:local, :rows]
    little = flat[LANES : LANES + 8, :rows]
    head_ref[...] = little[7:8, :each]
    hid_ref[...] = little[6:7, :]
    gain_ref[...] = little[0:2, :]
    bias_ref[...] = little[2:4, :]
    outb_ref[...] = little[4:6, :]


def body(
    frames, w_qkv, w_out, w_fc1, w_fc2, head_bias, hidden_bias, ln_gain, ln_bias, out_bias, cotangent
):
    n_f, n_c, n_t = lax.axis_size("fsdp"), lax.axis_size("ctx"), lax.axis_size("tp")
    _, length, width = frames.shape
    piece, local = w_qkv.shape[1], w_qkv.shape[2]
    blocks = n_f * n_c
    aligned = piece % 16 == 0
    f, t = lax.axis_index("fsdp"), lax.axis_index("tp")
    idx = jnp.stack([f, lax.axis_index("ctx"), t & 1, t]).astype(jnp.int32)
    x, cot = frames[0], cotangent[0]
    each = 2 * local // blocks
    place = np.zeros((width, 2 * LANES), np.float32)
    for b in range(blocks):
        for r in range(each):
            at = b * each + r
            place[b * piece + r, at % local + at // local * LANES] = 1
    place = jnp.asarray(place, BF)

    together = length // n_t == piece
    outs = (shape(piece, width + 128),) + (shape(piece, 2 * width + 128),) * together
    small = (ln_gain, ln_bias, out_bias, hidden_bias, head_bias)
    stay = (w_qkv, w_out, *small)
    first, *packet = call(
        first_kernel, outs, *stay, x,
        scratch=[pltpu.VMEM(a.shape, BF) for a in stay]
        + [pltpu.VMEM((length // n_t, width), BF), pltpu.SemaphoreType.DMA((len(stay) + 1,))],
        idx=idx, flops=10**9, where=pl.ANY, limit=60 * 1024 * 1024,
    )

    def near_blocks(shard):
        return [shard] + [send(shard, "ctx", k) for k in range(1, n_c)]

    def ordered(groups):
        if aligned:
            return groups
        groups = [jnp.concatenate([b if b.ndim == 3 else b[None] for b in g]) for g in groups]
        groups = jnp.stack(groups)
        return [[canonical(groups).reshape(1, width, -1)]]

    fc2_t = w_fc2.T
    own_far = [send(first, "fsdp", a) for a in range(1, n_f)]
    own1 = [send(after(w_fc1, first), "fsdp", a) for a in range(1, n_f)]
    if together:
        near = near_blocks(packet[0])[1:]
        near, far = [b[:, : first.shape[1]] for b in near], [b[:, first.shape[1] :] for b in near]
    else:
        quarter = lax.dynamic_slice_in_dim(x, t * (length // n_t), length // n_t, 0)
        near, far = near_blocks(first)[1:], near_blocks(quarter)[1:]
    near, far, own_far, own1 = lax.optimization_barrier((near, far, own_far, own1))
    far, rest = jnp.stack(far), jnp.stack(near)
    near = [first] + near
    rest_far = [send(rest, "fsdp", a) for a in range(1, n_f)]
    w_groups = ordered([near] + [[a, b] for a, b in zip(own_far, rest_far)])
    quarters = {0: far}
    bit = n_t // 2
    while bit > 0:
        for mask in list(quarters):
            quarters[mask ^ bit] = flip(quarters[mask], "tp", bit)
        bit //= 2
    quarters = {mask: [q] for mask, q in quarters.items()}
    masks = tuple(quarters)
    def sizes(groups):
        return tuple(len(g) for g in groups)

    def flat(groups):
        return [r for g in groups for r in g]

    halves = (shape(length // 2, width), shape(length // 2, width))
    rows_of = shape(length, LANES)
    w_all, wo, vec, n1, q_own, k_own, v_own = call(
        functools.partial(own_kernel, sizes(w_groups)),
        (
            shape(width, width + 128), shape(width, LANES), shape(8, width, dtype=F32),
            shape(length, width), rows_of, rows_of, rows_of,
        ),
        *flat(w_groups), x, place,
        idx=idx, flops=6 * 10**9,
    )
    near1 = [w_fc1] + near_blocks(after(w_fc1, far))[1:]
    rest1 = jnp.stack(after(near1[1:], vec))
    fc1 = ordered([near1] + [[a, send(rest1, "fsdp", k + 1)] for k, a in enumerate(own1)])
    own2 = [send(after(fc2_t, rest_far), "fsdp", a) for a in range(1, n_f)]
    near2 = [fc2_t] + near_blocks(after(fc2_t, rest1, quarters))[1:]
    rest2 = jnp.stack(near2[1:])
    fc2 = ordered([near2] + [[a, send(rest2, "fsdp", k + 1)] for k, a in enumerate(own2)])

    total = n_c * length
    every = shape(total, LANES)
    q_groups = list(quarters.values())
    q, k, v, o, aux, *branch = call(
        functools.partial(attend_kernel, masks, sizes(q_groups)),
        (every, every, every, shape(length, LANES, dtype=F32), rows_of, *halves),
        *flat(q_groups), w_all, wo, vec, place, after(q_own, rest1), k_own, v_own,
        scratch=[
            pltpu.VMEM((length, width), BF), pltpu.VMEM((length, width), BF),
            pltpu.VMEM((length, total), F32), pltpu.VMEM((length, LANES), F32),
        ],
        idx=idx, flops=14 * 10**9,
    )
    a0, a1 = tp_rest(tp_half((branch[0], after(branch[1], rest2, fc1, own2))))
    m, n2, g, df, mlp0, mlp1, dn0, dn1 = call(
        functools.partial(feed_kernel, sizes(fc1) + sizes(fc2)),
        (
            shape(length, width, dtype=F32), shape(length, width), shape(length, width),
            shape(length, width), *halves, *halves,
        ),
        *flat(fc1), *flat(fc2), x, a0, a1, cot, vec,
        scratch=[pltpu.VMEM((width, width), BF), pltpu.VMEM((width, width), BF)],
        idx=idx, flops=10 * 10**9,
    )
    dn_half = tp_half((dn0, dn1))

    def packed(cols):
        if aligned:
            return tuple(shape(n_c, piece, cols) for _ in range(n_f))
        return (shape(1, width, cols),)

    def as_blocks(parts):
        if aligned:
            return parts
        parts = relative(parts[0].reshape(n_f, n_c, piece, -1))
        return [parts[a] for a in range(n_f)]

    *gfc, hid = call(
        feed_grad_kernel,
        (*packed(width), *packed(width), shape(1, width, dtype=F32)),
        n2, after(df, dn_half), cot, g,
        scratch=[pltpu.VMEM((width, width), BF), pltpu.VMEM((width, width), BF)],
        idx=idx, flops=5 * 10**9,
    )
    first_half, second_half = [], []
    for a, part in list(enumerate(as_blocks(gfc[: len(gfc) // 2])))[1:]:
        first_half.append(send(part[: n_c // 2], "fsdp", a))
        second_half.append(send(part[n_c // 2 :], "fsdp", a))
    b0, b1 = tp_rest(dn_half, hid)
    b0, first_half = lax.optimization_barrier((b0, first_half))
    dm, da, pay, sent, sums2 = call(
        middle_kernel,
        (
            shape(length, width, dtype=F32), shape(length, width), shape(length, LANES),
            shape(SENT, length), shape(8, width, dtype=F32),
        ),
        m, b0, b1, cot, o, aux, wo, vec,
        idx=idx, flops=5 * 10**9,
    )
    far_pay = [send(sent, "ctx", j) for j in range(1, n_c)]

    def over_fsdp(parts):
        parts = as_blocks(parts)
        return [parts[0]] + [send(parts[a], "fsdp", a) for a in range(1, n_f)]

    def added(groups, wait, norm=None):
        groups = [[g[0], *after(g[1:], wait)] for g in groups]
        cols = sum(g[0].shape[-1] for g in groups)
        if not aligned:
            total = jnp.concatenate([sum(p.astype(F32) for p in g) for g in groups], axis=-1)
            if norm is not None:
                rows = relative(norm.T.reshape(n_f, n_c, piece, 8))[0]
                total = total.at[..., cols - 128 : cols - 120].add(rows)
            return list(total.astype(BF))
        extra = () if norm is None else (norm,)
        scratch = () if norm is None else (pltpu.VMEM((128, width), F32), pltpu.VMEM((width, 128), F32))
        return call(
            functools.partial(add_kernel, sizes(groups), norm is not None),
            tuple(shape(piece, cols) for _ in range(n_c)),
            *flat(groups), *extra,
            scratch=scratch, idx=idx, flops=10**9,
        )

    def over_ctx(low):
        return [low[0]] + [send(low[j], "ctx", j) for j in range(1, n_c)]

    def sum_of(parts):
        return sum(p.astype(F32) for p in parts)

    *gr_q, dq, dq_sum = call(
        query_kernel,
        (*packed(2 * local), rows_of, shape(8, LANES, dtype=F32)),
        q_own, pay, k, v, n1, da, o,
        scratch=[pltpu.VMEM((width, 2 * local), BF), pltpu.VMEM((DELTA // DH, length, LANES), F32)],
        idx=idx, flops=0,
    )
    gfc1 = as_blocks(gfc[: len(gfc) // 2])[:1]
    gfc1 += [jnp.concatenate(pair) for pair in zip(first_half, after(second_half, dq))]
    gfc2 = over_fsdp([after(p, gfc1) for p in gfc[len(gfc) // 2 :]])
    gfc1 = over_ctx(after(added([gfc1], dq), far_pay[0]))
    y0, y1 = tp_rest(tp_half((mlp0, after(mlp1, pay))))
    (dkv,) = call(
        functools.partial(key_kernel, n_c - 1),
        (shape(length, 3 * LANES),),
        *far_pay, k_own, v_own, q, after(pay, gfc1[0], y0), dq,
        scratch=[
            pltpu.VMEM((total, LANES), BF), pltpu.VMEM((total, LANES), BF),
            pltpu.VMEM((DELTA // DH, length, LANES), F32), pltpu.VMEM((DELTA // DH, length, LANES), F32),
        ],
        flops=12 * 10**9,
    )
    gr_q = over_fsdp([after(p, gfc2) for p in gr_q])
    grads = call(
        key_grad_kernel,
        packed(2 * local + 128),
        dkv, n1, sums2, hid, dq_sum, place,
        scratch=[pltpu.VMEM((width, 2 * local + 128), BF), pltpu.VMEM((128, width), F32)],
        idx=idx, flops=2 * 10**9,
    )
    dx0, dx1, sums1 = call(
        back_kernel, (*halves, shape(8, width, dtype=F32)), after(dkv, grads, gfc1, gfc2), w_all, x,
        idx=idx, flops=2 * 10**9,
    )
    grads = over_fsdp(grads)
    sums1 = sums_over(sums1, "tp")
    gfc2_low = added([gfc2], dx1)
    gfc2 = over_ctx(gfc2_low)
    sums1 = sums_over(after(sums1, gfc2_low, grads, gr_q), "fsdp")
    e_half = tp_half((dx0, dx1))
    rest = over_ctx(added([gr_q, grads], (gfc2), sums1))
    output = call(
        out_kernel, (shape(length, width),), m, y0, y1, vec, idx=idx, flops=2 * 10**9
    )[0]
    e0, e1 = tp_rest(e_half)
    input_grad = call(
        last_kernel, (shape(length, width),), x, e0, e1, dm, vec, idx=idx, flops=3 * 10**9
    )[0]

    fc1_grad, fc2_grad = sum_of(gfc1), sum_of(gfc2).T
    if aligned:
        qkv_grad, out_grad, head, hidden, gain, bias, outb = call(
            functools.partial(total_kernel, local, each),
            tuple(
                shape(*dims, dtype=F32)
                for dims in (
                    (3, piece, local), (local, piece), (1, each), (1, piece), (2, piece), (2, piece), (2, piece),
                )
            ),
            *rest,
            flops=2 * 10**9,
        )
    else:
        sums = sum_of(rest)
        cuts = [sums[:, j * local : (j + 1) * local] for j in range(4)]
        little = sums[:, 4 * local : 4 * local + 8].T
        qkv_grad, out_grad = jnp.stack([cuts[0], cuts[2], cuts[3]]), cuts[1].T
        head, hidden = little[7:8, :each], little[6:7]
        gain, bias, outb = little[0:2], little[2:4], little[4:6]
    return (
        output[None], input_grad[None], qkv_grad, out_grad, fc1_grad, fc2_grad, head, hidden, gain, bias, outb,
    )


def solution(mesh):
    shards = ("fsdp", "ctx")
    rows = P("fsdp", "ctx", None)
    qkv = P(None, shards, "tp")
    by_tp = P("tp", shards)
    norm = P(None, shards)
    weights = (qkv, by_tp, P(shards, "tp"), by_tp, by_tp, by_tp, norm, norm, norm)
    return jax.shard_map(
        body,
        mesh=mesh,
        in_specs=(rows, *weights, rows),
        out_specs=(rows, rows, *weights),
        check_vma=False,
    )
```
